32 devices in a mesh: groups: 2 (over y), dp: 4 (over z), replica: 2 (over x), mp: 2 (over core).
Axes of the slice: x: 2, y: 2, z: 4, core: 2. Of those that a mesh axis runs over, the one named last changes fastest.
Arguments:
- hot_slab: bfloat16 [16, 64, 128], P(None, 'mp'), may hold values from -1.5 to 1.5
- linear_state: float32 [16, 64, 128], P('dp', 'mp'), may hold values from -6 to 6
- square_state: float32 [16, 64, 128], P('dp', 'mp'), may hold values from 0.05 to 5
- serve_table: bfloat16 [2, 16, 64, 128], P('replica', 'dp', 'mp'), may hold values from -1.5 to 1.5
- first_weight: bfloat16 [16, 64, 512], P(None, 'mp'), may hold values from -0.1875 to 0.1875
- second_weight: bfloat16 [512, 256], replicated, may hold values from -0.25 to 0.25
- out_weight: bfloat16 [256], replicated, may hold values from -1.5 to 1.5
- step_blocks: int32 [4, 4], P('groups'), parts along dimension 0, may hold values from 0 to 15, as said below
- feature_ids: int32 [2, 4096, 16, 4], P(None, ('groups', 'dp', 'replica')), parts along dimension 1, may hold values from 0 to 511
- click_labels: float32 [2, 4096], P(None, ('groups', 'dp', 'replica')), parts along dimension 1, may hold values from 0 to 1
- serve_layout: int32 [2, 4], P('replica'), may hold values from 0 to 3, each once within a row
- request_ids: int32 [2, 64, 16, 4], P('replica', ('groups', 'dp')), parts along dimension 1, may hold values from 0 to 2047
Outputs:
- new_linear: float32 [32, 64, 128], P(('groups', 'dp'), 'mp'), parts along dimension 0
- new_square: float32 [32, 64, 128], P(('groups', 'dp'), 'mp'), parts along dimension 0
- new_serve: bfloat16 [4, 16, 64, 128], P(('groups', 'replica'), 'dp', 'mp'), parts along dimension 0
- request_scores: float32 [2, 64], P('replica', ('groups', 'dp')), parts along dimension 1
The draws below stay inside these ranges and needn't reach their ends.
There are 2 independent parts, one for each index of `groups`. The reference program is written for one: setup_inputs(seed, part) draws one part's arguments, and reference() takes and returns one part's arrays. A program takes and returns all parts, laid end to end along the dimension named above; an argument that names none is the same for every part. Nothing has to cross between parts.
Inputs may be any that keep to these rules, and one draw needn't show every extreme that they name: `step_blocks`: the blocks of one step are distinct; the last 2 blocks of step t are the first 2 of step t + 1. `serve_layout`: each row names every owner once.
All inputs are finite; a program needn't handle non-finite values.
Results may differ from the reference program's by a relative error of at most 0.011.
Values may be sent and summed in bfloat16 or wider, within the bound.
No kernel may reach another device: no remote copies, remote signals or barrier semaphores. Data moves between devices by JAX's collectives and lax.ppermute only.
A program may use at most 64 MiB of HBM per device.

```python
import math
import jax
import jax.numpy as jnp
import numpy as np
from jax import lax

EMB = 64
SLOTS = 16
IDS_SLOT = 4
H1 = 512
H2 = 256
BLOCK_ROWS = 128
HBD = 4
STEPS = 2
HB = 16
ACT = 4
BATCH = 2048
SREQ = 32
N_DP = 4
N_REPLICA = 2


def draw_step_blocks(key, part):
    key = jax.random.fold_in(key, 11)
    ordering = jax.random.permutation(key, HB).astype(jnp.int32)
    starts = jnp.arange(STEPS, dtype=jnp.int32) * (ACT // 2)
    picks = starts[:, None] + jnp.arange(ACT, dtype=jnp.int32)[None, :]
    return jnp.take(ordering, picks)


def set_ends(entries, stream_key, smallest, largest):
    longest = entries.shape.index(max(entries.shape))
    spots = []
    for shift in (0, 1):
        where = [jax.random.randint(jax.random.fold_in(stream_key, axis), (), 0, length) for axis, length in enumerate(entries.shape)]
        where[longest] = (where[longest] + shift) % entries.shape[longest]
        spots.append(tuple(where))
    return entries.at[spots[0]].set(smallest).at[spots[1]].set(largest)


def block_levels(own_key, shape, shards, low, high):
    factor_of, own = 1.0, jax.random.fold_in(own_key, 6)
    for axis_at, shards_of in shards:
        heights = jnp.exp(jax.random.uniform(jax.random.fold_in(own, axis_at), (shards_of,), jnp.float32, low / len(shards), high / len(shards)))
        factor_of = factor_of * jnp.repeat(heights, shape[axis_at] // shards_of).reshape([-1 if axis == axis_at else 1 for axis in range(len(shape))])
    return factor_of


def rank_bounds(amount, lean):
    portions = [(1 << 20) // math.isqrt(grade ** lean) + 1 for grade in range(1, amount + 1)]
    scale = 1 + sum(portions) // (1 << 30)
    return np.cumsum(np.array([max(1, weight // scale) for weight in portions]))


def ranked_ids(own_key, dims, number_of, slope):
    listing = rank_bounds(number_of, slope)
    ticket = jax.random.randint(jax.random.fold_in(own_key, 1), dims, 0, int(listing[number_of - 1]))
    grade = jnp.searchsorted(jnp.asarray(listing, jnp.int32), ticket, side="right")
    return jax.random.permutation(jax.random.fold_in(own_key, 2), number_of)[grade].astype(jnp.int32)


def gaussian(key, shape, deviation, most, pieces=(), held_as=jnp.bfloat16):
    values = deviation * jax.random.normal(key, shape, jnp.float32)
    if pieces:
        values = values * block_levels(key, shape, pieces, -0.22, 0.18)
    return jnp.clip(values, -most, most).astype(held_as)


def setup_inputs(seed: int = 0, part: int = 0) -> dict:
    streams_of = jax.random.split(jax.random.key(seed), 13)
    own_keys = jax.random.split(jax.random.fold_in(streams_of[12], part), 13)
    hot_slab = gaussian(streams_of[0], (HB, EMB, BLOCK_ROWS), 0.25, 1.5, ((1, 2),))
    linear_state = gaussian(streams_of[1], (HB, EMB, BLOCK_ROWS), 1.0, 6.0, ((0, 4), (1, 2)), jnp.float32)
    square_state = jnp.clip(jnp.exp(math.log(5.0) - 4.6051702 * jax.random.uniform(streams_of[2], (HB, EMB, BLOCK_ROWS), jnp.float32) ** block_levels(streams_of[2], (HB, EMB, BLOCK_ROWS), ((0, 4), (1, 2)), -0.2, 0.2)), 0.05, 5.0)
    serve_table = gaussian(streams_of[3], (N_REPLICA, HB, EMB, BLOCK_ROWS), 0.25, 1.5, ((0, 2), (1, 4), (2, 2)))
    first_weight = gaussian(streams_of[4], (SLOTS, EMB, H1), (SLOTS * EMB) ** -0.5, 0.1875, ((1, 2),))
    second_weight = gaussian(streams_of[5], (H1, H2), H1 ** -0.5, 0.25)
    out_weight = gaussian(streams_of[6], (H2,), 0.25, 1.5)
    step_blocks = draw_step_blocks(jax.random.fold_in(jax.random.fold_in(streams_of[12], part), 71), part)
    feature_ids = set_ends(ranked_ids(own_keys[8], (STEPS, BATCH, SLOTS, IDS_SLOT), ACT * BLOCK_ROWS, 1), jax.random.fold_in(own_keys[8], 3), 0, (ACT * BLOCK_ROWS) - 1).astype(jnp.int32)
    click_labels = jnp.clip(1.0 * jax.random.uniform(own_keys[9], (STEPS, BATCH), jnp.float32) ** block_levels(own_keys[9], (STEPS, BATCH), ((1, 8),), -0.2, 0.2), 0.0, 1.0)
    serve_layout = jax.vmap(lambda own: jax.random.permutation(own, N_DP))(jax.random.split(streams_of[10], N_REPLICA)).reshape((N_REPLICA, N_DP)).astype(jnp.int32)
    request_ids = set_ends(jax.random.randint(own_keys[11], (N_REPLICA, SREQ, SLOTS, IDS_SLOT), 0, HB * BLOCK_ROWS), jax.random.fold_in(own_keys[11], 1), 0, (HB * BLOCK_ROWS) - 1).astype(jnp.int32)
    return {"hot_slab": hot_slab, "linear_state": linear_state, "square_state": square_state, "serve_table": serve_table, "first_weight": first_weight, "second_weight": second_weight, "out_weight": out_weight, "step_blocks": step_blocks, "feature_ids": feature_ids, "click_labels": click_labels, "serve_layout": serve_layout, "request_ids": request_ids}


step_alpha = 0.5
step_beta = 1.0
sparse_penalty = 0.1
ridge_penalty = 0.05

def silu_slope(inputs):
    logistic = jax.nn.sigmoid(inputs)
    return logistic * (1.0 + inputs * (1.0 - logistic))

def ftrl_update(linear, square, gradient, current):
    grown = square + gradient * gradient
    sigma_term = (jnp.sqrt(grown) - jnp.sqrt(square)) / step_alpha
    linear_next = linear + gradient - sigma_term * current
    shrunk = linear_next - jnp.clip(linear_next, -sparse_penalty, sparse_penalty)
    weights = -shrunk / ((step_beta + jnp.sqrt(grown)) / step_alpha + ridge_penalty)
    return (linear_next, grown, weights)

def block_table(blocks):
    return jnp.transpose(blocks, (0, 2, 1)).reshape(-1, blocks.shape[1]).astype(jnp.float32)

def forward_pass(pooled, first_weight, second_weight, out_weight):
    first_flat = first_weight.reshape(-1, first_weight.shape[2])
    flattened = pooled.reshape(pooled.shape[0], -1)
    hidden_pre = jnp.dot(flattened, first_flat, preferred_element_type=jnp.float32)
    hidden_one = jax.nn.silu(hidden_pre).astype(jnp.bfloat16)
    second_pre = jnp.dot(hidden_one, second_weight, preferred_element_type=jnp.float32)
    hidden_two = jax.nn.silu(second_pre).astype(jnp.bfloat16)
    logits = jnp.dot(hidden_two, out_weight, preferred_element_type=jnp.float32)
    return (hidden_pre, second_pre, logits)

def reference(hot_slab, linear_state, square_state, serve_table, first_weight, second_weight, out_weight, step_blocks, feature_ids, click_labels, serve_layout, request_ids):
    current_slab = hot_slab
    linear = linear_state
    square = square_state
    first_flat = first_weight.reshape(-1, first_weight.shape[2])
    for step_index in range(STEPS):
        chosen = step_blocks[step_index]
        active = current_slab[chosen]
        lookup = block_table(active)
        step_ids = feature_ids[step_index]
        pooled = lax.optimization_barrier(jnp.sum(lookup[step_ids], axis=2)).astype(jnp.bfloat16)
        hidden_pre, second_pre, logits = forward_pass(pooled, first_weight, second_weight, out_weight)
        logit_error = jax.nn.sigmoid(logits) - click_labels[step_index]
        grad_two = (logit_error[:, None] * out_weight.astype(jnp.float32)[None, :] * silu_slope(second_pre)).astype(jnp.bfloat16)
        back_one = jnp.dot(grad_two, second_weight.T, preferred_element_type=jnp.float32)
        grad_one = (back_one * silu_slope(hidden_pre)).astype(jnp.bfloat16)
        grad_input = jnp.dot(grad_one, first_flat.T, preferred_element_type=jnp.float32).astype(jnp.bfloat16)
        grad_input = grad_input.reshape(BATCH, SLOTS, EMB).astype(jnp.float32)
        spread = jnp.broadcast_to(grad_input[:, :, None, :], (BATCH, SLOTS, IDS_SLOT, EMB))
        rows_grad = jnp.zeros((ACT * BLOCK_ROWS, EMB), jnp.float32).at[step_ids.reshape(-1)].add(spread.reshape(-1, EMB))
        gradient = jnp.transpose(rows_grad.reshape(ACT, BLOCK_ROWS, EMB), (0, 2, 1))
        linear_next, square_next, weights = ftrl_update(linear[chosen], square[chosen], gradient, active.astype(jnp.float32))
        linear = linear.at[chosen].set(linear_next)
        square = square.at[chosen].set(square_next)
        current_slab = current_slab.at[chosen].set(weights.astype(jnp.bfloat16))
    block_range = jnp.arange(HB, dtype=jnp.int32)
    touched = jnp.any(step_blocks.reshape(-1)[None, :] == block_range[:, None], axis=1)
    owner_of = block_range // HBD
    slot_of = block_range % HBD
    owner_range = jnp.arange(N_DP, dtype=jnp.int32)
    served_tables = []
    scores = []
    for replica_index in range(N_REPLICA):
        layout = serve_layout[replica_index]
        inverse = lax.optimization_barrier(jnp.sum(jnp.where(layout[:, None] == owner_range[None, :], owner_range[:, None], 0), axis=0)).astype(jnp.int32)
        source = (inverse[owner_of] - slot_of) % N_DP
        block_of = (source * HBD + slot_of).astype(jnp.int32)
        refreshed = jnp.where(touched[block_of][:, None, None], current_slab[block_of], serve_table[replica_index])
        served_tables.append(refreshed)
        lookup = block_table(refreshed)
        served = lax.optimization_barrier(jnp.sum(lookup[request_ids[replica_index]], axis=2)).astype(jnp.bfloat16)
        unused_one, unused_two, logits = forward_pass(served, first_weight, second_weight, out_weight)
        scores.append(logits)
    return (linear, square, jnp.stack(served_tables), jnp.stack(scores))
```

```python
import functools

import jax
import jax.numpy as jnp
from jax import lax
from jax.experimental import pallas as pl
from jax.experimental.pallas import tpu as pltpu
from jax.sharding import PartitionSpec as P

step_alpha = 0.5
step_beta = 1.0
sparse_penalty = 0.1
ridge_penalty = 0.05
f32 = jnp.float32
bf16 = jnp.bfloat16
VMEM = pl.BlockSpec(memory_space=pltpu.VMEM)
SMEM = pl.BlockSpec(memory_space=pltpu.SMEM)
nt_dims = (((1,), (1,)), ((), ()))


def kernel_call(body, out_shape, in_specs, scratch=(), limit=48):
    return pl.pallas_call(
        body,
        out_shape=out_shape,
        in_specs=in_specs,
        out_specs=jax.tree.map(lambda _: VMEM, out_shape),
        scratch_shapes=list(scratch),
        compiler_params=pltpu.CompilerParams(vmem_limit_bytes=limit * 1024 * 1024),
    )


def sigmoid(v):
    return 1.0 / (1.0 + jnp.exp(-v))


def ftrl_update(linear, square, gradient, current):
    grown = square + gradient * gradient
    root = jnp.sqrt(grown)
    sigma_term = (root - jnp.sqrt(square)) / step_alpha
    linear_next = linear + gradient - sigma_term * current
    shrunk = linear_next - jnp.clip(linear_next, -sparse_penalty, sparse_penalty)
    weights = -shrunk / ((step_beta + root) / step_alpha + ridge_penalty)
    return linear_next, grown, weights


def fill_counts(counts_ref, lanes_ids, column, blocks, rows):
    picks, lanes = lanes_ids.shape
    tiles = rows // 16
    level = lax.broadcasted_iota(jnp.int32, (tiles, 16, lanes), 1) + 16 * lax.broadcasted_iota(
        jnp.int32, (tiles, 16, lanes), 0
    )
    level = level.astype(bf16)
    one = jnp.ones((), bf16)
    zero = jnp.zeros((), bf16)
    for block in range(blocks):
        rel = jnp.clip(lanes_ids - block * rows, -1, rows)
        total = None
        for pick in range(picks):
            wide = jnp.broadcast_to(rel[pick : pick + 1], (16, lanes)).astype(f32).astype(bf16)
            hit = jnp.where(level == wide[None], one, zero)
            total = hit if total is None else total + hit
        counts_ref[block * rows : (block + 1) * rows, column : column + lanes] = total.reshape(
            rows, lanes
        )


def step_body(
    step,
    samples,
    ids_ref,
    labels_ref,
    table_own,
    table_other,
    w1_own,
    w1_other,
    w2_ref,
    wout_ref,
    counts_ref,
    active,
    rows,
):
    core = lax.axis_index("mp")
    slots = ids_ref.shape[1]
    half = table_own.shape[0]
    lanes = pl.ds(pl.multiple_of(core * samples, samples), samples)
    for slot in range(slots):
        fill_counts(counts_ref, ids_ref[step, slot, :, lanes], slot * samples, active, rows)
    counts = counts_ref[...]
    table = jnp.concatenate([table_own, table_other], axis=0)
    pooled = jnp.dot(table, counts, preferred_element_type=f32)

    def by_sample(low):
        stacked = jnp.concatenate(
            [
                pooled[low : low + half, slot * samples : (slot + 1) * samples]
                for slot in range(slots)
            ],
            axis=0,
        )
        return stacked.T.astype(bf16)

    first_own = w1_own[...]
    first_other = w1_other[...]
    pre_one = jnp.dot(by_sample(0), first_own, preferred_element_type=f32) + jnp.dot(
        by_sample(half), first_other, preferred_element_type=f32
    )
    sig_one = sigmoid(pre_one)
    hidden_one = (pre_one * sig_one).astype(bf16)
    second = w2_ref[...]
    pre_two = jnp.dot(hidden_one, second, preferred_element_type=f32)
    sig_two = sigmoid(pre_two)
    hidden_two = (pre_two * sig_two).astype(bf16).astype(f32)
    head = wout_ref[...].astype(f32)
    logit = jnp.sum(hidden_two * head, axis=1, keepdims=True)
    label_row = labels_ref[step : step + 1, lanes]
    label = jnp.broadcast_to(label_row, (samples, samples)).T[:, 0:1]
    error = sigmoid(logit) - label
    grad_two = (error * head * (sig_two * (1.0 + pre_two * (1.0 - sig_two)))).astype(bf16)
    back = lax.dot_general(grad_two, second, nt_dims, preferred_element_type=f32)
    grad_one = (back * (sig_one * (1.0 + pre_one * (1.0 - sig_one)))).astype(bf16)

    def by_column(first):
        spread = lax.dot_general(first, grad_one, nt_dims, preferred_element_type=f32).astype(bf16)
        return jnp.concatenate(
            [spread[slot * half : (slot + 1) * half] for slot in range(slots)], axis=1
        )

    grad_input = jnp.concatenate([by_column(first_own), by_column(first_other)], axis=0)
    return lax.dot_general(grad_input, counts, nt_dims, preferred_element_type=f32)


def first_step_kernel(
    samples,
    blocks_ref,
    ids_ref,
    labels_ref,
    slab_own,
    slab_other,
    w1_own,
    w1_other,
    w2_ref,
    wout_ref,
    share_own,
    share_other,
    rest_own,
    rest_other,
    counts_ref,
):
    active = blocks_ref.shape[1]
    rows = slab_own.shape[2]
    half = slab_own.shape[1]
    fresh = active // 2
    chosen = [blocks_ref[0, i] for i in range(active)]
    grad = step_body(
        0,
        samples,
        ids_ref,
        labels_ref,
        jnp.concatenate([slab_own[c] for c in chosen], axis=1),
        jnp.concatenate([slab_other[c] for c in chosen], axis=1),
        w1_own,
        w1_other,
        w2_ref,
        wout_ref,
        counts_ref,
        active,
        rows,
    )
    for i in range(active):
        part = grad[:, i * rows : (i + 1) * rows].astype(bf16)
        own, other, at = (rest_own, rest_other, i) if i < fresh else (share_own, share_other, i - fresh)
        own[at] = part[:half]
        other[at] = part[half:]


def second_step_kernel(
    samples,
    blocks_ref,
    ids_ref,
    labels_ref,
    slab_own,
    slab_other,
    new_own,
    new_other,
    rest_own,
    rest_other,
    w1_own,
    w1_other,
    w2_ref,
    wout_ref,
    out_own,
    out_other,
    counts_ref,
):
    active = blocks_ref.shape[1]
    rows = slab_own.shape[2]
    half = slab_own.shape[1]
    fresh = active // 2

    def tables(shared, slab):
        return jnp.concatenate(
            [shared[i] for i in range(fresh)] + [slab[blocks_ref[1, i]] for i in range(fresh, active)],
            axis=1,
        )

    grad = step_body(
        1,
        samples,
        ids_ref,
        labels_ref,
        tables(new_own, slab_own),
        tables(new_other, slab_other),
        w1_own,
        w1_other,
        w2_ref,
        wout_ref,
        counts_ref,
        active,
        rows,
    )
    out_own[0:fresh] = rest_own[...]
    out_other[0:fresh] = rest_other[...]
    for i in range(active):
        part = grad[:, i * rows : (i + 1) * rows].astype(bf16)
        out_own[fresh + i] = part[:half]
        out_other[fresh + i] = part[half:]


def pack_kernel(linear_ref, square_ref, serve_ref, out_ref):
    owned = linear_ref.shape[0]
    linear = linear_ref[...]
    high = linear.astype(bf16)
    out_ref[0:owned] = high
    out_ref[owned : 2 * owned] = (linear - high.astype(f32)).astype(bf16)
    out_ref[2 * owned : 3 * owned] = square_ref[...].astype(bf16)
    out_ref[3 * owned : 4 * owned] = serve_ref[...]


def tree_sum(parts):
    parts = list(parts)
    while len(parts) > 1:
        parts = [
            parts[i] + parts[i + 1] if i + 1 < len(parts) else parts[i]
            for i in range(0, len(parts), 2)
        ]
    return parts[0]


def fetch_state(block, me, linear_ref, square_ref, packs, linear_at, square_at, at):
    owned = linear_ref.shape[0]
    owner = block // owned
    place = block % owned

    @pl.when(owner == me)
    def _():
        linear_at[at] = linear_ref[place]
        square_at[at] = square_ref[place]

    def take(piece):
        linear_at[at] = piece(place).astype(f32) + piece(owned + place).astype(f32)
        square_at[at] = piece(2 * owned + place).astype(f32)

    if len(packs) == 1:

        @pl.when(owner != me)
        def _():
            take(lambda i: packs[0][owner, i])

    else:
        for k, pack in enumerate(packs):

            @pl.when((owner ^ me) == k + 1)
            def _():
                take(lambda i: pack[i])


def share_kernel(sums_count, packs_count, *refs):
    blocks_ref, linear_ref, square_ref, slab_own = refs[:4]
    sums = refs[4 : 4 + sums_count]
    packs = refs[4 + sums_count : 4 + sums_count + packs_count]
    new_own, linear_out, square_out, linear_at, square_at = refs[4 + sums_count + packs_count :]
    active = blocks_ref.shape[1]
    fresh = active // 2
    me = lax.axis_index("dp")
    for i in range(active - fresh):
        block = blocks_ref[0, fresh + i]
        fetch_state(block, me, linear_ref, square_ref, packs, linear_at, square_at, i)
        gradient = tree_sum([part[i].astype(f32) for part in sums])
        linear, square, weights = ftrl_update(
            linear_at[i], square_at[i], gradient, slab_own[block].astype(f32)
        )
        linear_out[i] = linear
        square_out[i] = square
        new_own[i] = weights.astype(bf16)


def finish_kernel(owners, sums_count, packs_count, *refs):
    blocks_ref, layout_ref, req_ref, linear_ref, square_ref, serve_ref, slab_own = refs[:7]
    new_own, linear_mid, square_mid, w1_own = refs[7:11]
    sums = refs[11 : 11 + sums_count]
    packs = refs[11 + sums_count : 11 + sums_count + packs_count]
    linear_out, square_out, serve_out, partial_out = refs[11 + sums_count + packs_count :][:4]
    table_at, counts_ref, linear_at, square_at = refs[11 + sums_count + packs_count + 4 :]
    active = blocks_ref.shape[1]
    owned, half, rows = linear_ref.shape
    fresh = active // 2
    me = lax.axis_index("dp")
    for k in range(owners):
        if len(packs) == 1:
            table_at[k * owned : (k + 1) * owned] = packs[0][k, 3 * owned : 4 * owned]
        elif k == 0:
            table_at[pl.ds(me * owned, owned)] = serve_ref[...]
        else:
            table_at[pl.ds((me ^ k) * owned, owned)] = packs[k - 1][3 * owned : 4 * owned]
    linear_out[...] = linear_ref[...]
    square_out[...] = square_ref[...]
    serve_out[...] = serve_ref[...]
    for i in range(active + fresh):
        block = blocks_ref[0, i] if i < fresh else blocks_ref[1, i - fresh]
        gradient = tree_sum([part[i].astype(f32) for part in sums])
        if fresh <= i < active:
            linear_old = linear_mid[i - fresh]
            square_old = square_mid[i - fresh]
            current = new_own[i - fresh]
        else:
            fetch_state(block, me, linear_ref, square_ref, packs, linear_at, square_at, i)
            linear_old = linear_at[i]
            square_old = square_at[i]
            current = slab_own[block]
        linear, square, weights = ftrl_update(
            linear_old, square_old, gradient, current.astype(f32)
        )
        weights = weights.astype(bf16)
        owner = block // owned
        place = block % owned
        target = layout_ref[0, (owner + place) % owners]
        table_at[target * owned + place] = weights

        @pl.when(owner == me)
        def _():
            linear_out[place] = linear
            square_out[place] = square

        @pl.when(target == me)
        def _():
            serve_out[place] = weights

    requests, picks, slots = req_ref.shape
    lanes = requests * slots
    lanes_ids = jnp.concatenate([req_ref[i] for i in range(requests)], axis=1)
    positions = owners * owned
    fill_counts(counts_ref, lanes_ids, 0, positions, rows)
    table = jnp.concatenate([table_at[i] for i in range(positions)], axis=1)
    pooled = jnp.dot(table, counts_ref[...], preferred_element_type=f32)
    stacked = jnp.concatenate([pooled] * slots, axis=0)
    wanted = lax.broadcasted_iota(jnp.int32, stacked.shape, 0) // half
    present = lax.broadcasted_iota(jnp.int32, stacked.shape, 1) % slots
    stacked = jnp.where(wanted == present, stacked, 0.0)
    product = jnp.dot(stacked.T.astype(bf16), w1_own[...], preferred_element_type=f32)
    partial_out[...] = jnp.sum(product.reshape(requests, slots, product.shape[1]), axis=1)


def score_kernel(own_ref, other_ref, w2_ref, wout_ref, out_ref):
    pre_one = own_ref[...] + other_ref[...]
    hidden_one = (pre_one * sigmoid(pre_one)).astype(bf16)
    pre_two = jnp.dot(hidden_one, w2_ref[...], preferred_element_type=f32)
    hidden_two = (pre_two * sigmoid(pre_two)).astype(bf16).astype(f32)
    logit = jnp.sum(hidden_two * wout_ref[...].astype(f32), axis=1, keepdims=True)
    out_ref[...] = logit


def swap(value, axes, sizes, bits):
    shape = tuple(sizes[a] for a in axes)
    count = 1
    for size in shape:
        count *= size
    pairs = []
    for index in range(count):
        rest, coords = index, []
        for size in reversed(shape):
            coords.append(rest % size)
            rest //= size
        coords = coords[::-1]
        target = 0
        for coord, bit, size in zip(coords, bits, shape):
            target = target * size + (coord ^ bit)
        pairs.append((index, target))
    return lax.ppermute(value, axes, pairs)


def reduce_halves(own, other, sizes):
    def add(parts):
        return tree_sum([p.astype(f32) for p in parts]).astype(bf16)

    replicas, owners = sizes["replica"], sizes["dp"]
    parts = [own]
    if replicas > 1:
        parts = [
            own,
            swap(own, ("replica", "mp"), sizes, (1, 0)),
            swap(other, ("replica", "mp"), sizes, (0, 1)),
            swap(other, ("replica", "mp"), sizes, (1, 1)),
        ]
    else:
        parts = [own, swap(other, ("mp",), sizes, (1,))]
    bit = 2
    while bit < replicas:
        total = add(parts)
        parts = [total, swap(total, ("replica",), sizes, (bit,))]
        bit *= 2
    bit = 1
    while bit < owners:
        total = add(parts)
        steps = [k * bit for k in range(1, 4) if k * bit < owners]
        parts = [total] + [swap(total, ("dp",), sizes, (k,)) for k in steps]
        bit *= 4
    return parts


def local(
    sizes,
    hot_slab,
    linear_state,
    square_state,
    serve_table,
    first_weight,
    second_weight,
    out_weight,
    step_blocks,
    feature_ids,
    click_labels,
    serve_layout,
    request_ids,
):
    owners = sizes["dp"]
    owned, half, rows = linear_state.shape
    active = step_blocks.shape[1]
    fresh = active // 2
    samples = feature_ids.shape[1] // sizes["mp"]
    slots = feature_ids.shape[2]
    units = first_weight.shape[2]
    ids = jnp.transpose(feature_ids, (0, 2, 3, 1))
    req = jnp.transpose(request_ids[0], (0, 2, 1))
    w1_own = first_weight.reshape(-1, units)
    w1_other = swap(w1_own, ("mp",), sizes, (1,))
    slab_other = swap(hot_slab, ("mp",), sizes, (1,))
    head = out_weight.reshape(1, -1)
    serve_own = serve_table[0]

    pack = kernel_call(
        pack_kernel, jax.ShapeDtypeStruct((4 * owned, half, rows), bf16), [VMEM] * 3
    )(linear_state, square_state, serve_own)
    if owners == 4:
        packs = [swap(pack, ("dp",), sizes, (k,)) for k in range(1, owners)]
    else:
        packs = [lax.all_gather(pack, "dp", axis=0, tiled=False)]

    counts = pltpu.VMEM((active * rows, slots * samples), bf16)
    halves = jax.ShapeDtypeStruct((fresh, half, rows), bf16)
    shared = jax.ShapeDtypeStruct((active - fresh, half, rows), bf16)
    share_own, share_other, rest_own, rest_other = kernel_call(
        functools.partial(first_step_kernel, samples),
        (shared, shared, halves, halves),
        [SMEM] + [VMEM] * 8,
        [counts],
    )(
        step_blocks,
        ids,
        click_labels,
        hot_slab,
        slab_other,
        w1_own,
        w1_other,
        second_weight,
        head,
    )
    sums = reduce_halves(share_own, share_other, sizes)
    state = jax.ShapeDtypeStruct((active - fresh, half, rows), f32)
    state_at = pltpu.VMEM((active + fresh, half, rows), f32)
    new_own, linear_mid, square_mid = kernel_call(
        functools.partial(share_kernel, len(sums), len(packs)),
        (shared, state, state),
        [SMEM] + [VMEM] * (3 + len(sums) + len(packs)),
        [state_at, state_at],
    )(step_blocks, linear_state, square_state, hot_slab, *sums, *packs)
    new_other = swap(new_own, ("mp",), sizes, (1,))

    payload = jax.ShapeDtypeStruct((active + fresh, half, rows), bf16)
    grad_own, grad_other = kernel_call(
        functools.partial(second_step_kernel, samples),
        (payload, payload),
        [SMEM] + [VMEM] * 12,
        [counts],
    )(
        step_blocks,
        ids,
        click_labels,
        hot_slab,
        slab_other,
        new_own,
        new_other,
        rest_own,
        rest_other,
        w1_own,
        w1_other,
        second_weight,
        head,
    )
    sums = reduce_halves(grad_own, grad_other, sizes)
    requests = req.shape[0]
    positions = owners * owned
    linear_out, square_out, serve_out, partial = kernel_call(
        functools.partial(finish_kernel, owners, len(sums), len(packs)),
        (
            jax.ShapeDtypeStruct(linear_state.shape, f32),
            jax.ShapeDtypeStruct(square_state.shape, f32),
            jax.ShapeDtypeStruct(serve_own.shape, bf16),
            jax.ShapeDtypeStruct((requests, units), f32),
        ),
        [SMEM, SMEM] + [VMEM] * (9 + len(sums) + len(packs)),
        [
            pltpu.VMEM((positions, half, rows), bf16),
            pltpu.VMEM((positions * rows, requests * slots), bf16),
            state_at,
            state_at,
        ],
    )(
        step_blocks,
        serve_layout,
        req,
        linear_state,
        square_state,
        serve_own,
        hot_slab,
        new_own,
        linear_mid,
        square_mid,
        w1_own,
        *sums,
        *packs,
    )
    partial_other = swap(partial, ("mp",), sizes, (1,))
    scores = kernel_call(score_kernel, jax.ShapeDtypeStruct((requests, 1), f32), [VMEM] * 4)(
        partial, partial_other, second_weight, head
    )
    return linear_out, square_out, serve_out[None], scores.reshape(1, requests)


def solution(mesh):
    sizes = dict(mesh.shape)
    placed = (
        P(None, "mp", None),
        P("dp", "mp", None),
        P("dp", "mp", None),
        P("replica", "dp", "mp", None),
        P(None, "mp", None),
        P(),
        P(),
        P("groups", None),
        P(None, ("groups", "dp", "replica"), None, None),
        P(None, ("groups", "dp", "replica")),
        P("replica", None),
        P("replica", ("groups", "dp"), None, None),
    )
    return jax.shard_map(
        functools.partial(local, sizes),
        mesh=mesh,
        in_specs=placed,
        out_specs=(
            P(("groups", "dp"), "mp", None),
            P(("groups", "dp"), "mp", None),
            P(("groups", "replica"), "dp", "mp", None),
            P("replica", ("groups", "dp")),
        ),
        check_vma=False,
    )
```

```python
import functools

import jax
import jax.numpy as jnp
from jax import lax
from jax.experimental import pallas as pl
from jax.experimental.pallas import tpu as pltpu
from jax.sharding import PartitionSpec as P

step_alpha = 0.5
step_beta = 1.0
sparse_penalty = 0.1
ridge_penalty = 0.05
share_owners = False
micros_default = 1.0
f32 = jnp.float32
bf16 = jnp.bfloat16
VMEM = pl.BlockSpec(memory_space=pltpu.VMEM)
HBM = pl.BlockSpec(memory_space=pltpu.HBM)
SMEM = pl.BlockSpec(memory_space=pltpu.SMEM)
nt_dims = (((1,), (1,)), ((), ()))


def kernel_call(body, out_shape, in_specs, scratch=(), out_specs=None, micros=micros_default, limit=32):
    return pl.pallas_call(
        body,
        out_shape=out_shape,
        in_specs=in_specs,
        out_specs=jax.tree.map(lambda _: VMEM, out_shape) if out_specs is None else out_specs,
        scratch_shapes=list(scratch),
        compiler_params=pltpu.CompilerParams(vmem_limit_bytes=limit * 1024 * 1024),
        cost_estimate=pl.CostEstimate(
            flops=int(micros * 1e9), bytes_accessed=int(micros * 1e6), transcendentals=0
        ),
    )


def sigmoid(v):
    return 1.0 / (1.0 + jnp.exp(-v))


def ftrl_update(linear, square, gradient, current):
    grown = square + gradient * gradient
    root = jnp.sqrt(grown)
    sigma_term = (root - jnp.sqrt(square)) / step_alpha
    linear_next = linear + gradient - sigma_term * current
    shrunk = linear_next - jnp.clip(linear_next, -sparse_penalty, sparse_penalty)
    weights = -shrunk / ((step_beta + root) / step_alpha + ridge_penalty)
    return linear_next, grown, weights


def fill_counts(counts_ref, ids, column, blocks, rows):
    picks, lanes = ids.shape
    tiles = rows // 16
    level = lax.broadcasted_iota(jnp.int32, (tiles, 16, lanes), 1) + 16 * lax.broadcasted_iota(
        jnp.int32, (tiles, 16, lanes), 0
    )
    level = level.astype(f32).astype(bf16)
    wide = [jnp.broadcast_to(ids[pick : pick + 1], (16, lanes)) for pick in range(picks)]
    times = []
    for pick in range(picks):
        total = jnp.ones((16, lanes), f32)
        for later in range(pick + 1, picks):
            total = total + jnp.where(wide[later] == wide[pick], 1.0, 0.0)
        times.append(total.astype(bf16)[None])
    zero = jnp.zeros((), bf16)
    for block in range(blocks):
        filled = None
        for pick in reversed(range(picks)):
            place = (wide[pick] - float(block * rows)).astype(bf16)[None]
            filled = jnp.where(level == place, times[pick], zero if filled is None else filled)
        counts_ref[block * rows : (block + 1) * rows, column : column + lanes] = filled.reshape(
            rows, lanes
        )


def tree_sum(parts):
    parts = list(parts)
    while len(parts) > 1:
        parts = [
            parts[i] + parts[i + 1] if i + 1 < len(parts) else parts[i]
            for i in range(0, len(parts), 2)
        ]
    return parts[0]


def step_body(table, counts, label_row, w1_own, w1_other, w2_ref, head_ref, slots):
    half = table.shape[0] // 2
    samples = counts.shape[1] // slots
    pooled = jnp.dot(table, counts, preferred_element_type=f32)

    def by_sample(low):
        stacked = jnp.concatenate(
            [
                pooled[low : low + half, slot * samples : (slot + 1) * samples]
                for slot in range(slots)
            ],
            axis=0,
        )
        return stacked.T.astype(bf16)

    first_own, first_other, second = w1_own[...], w1_other[...], w2_ref[...]
    pre_one = jnp.dot(by_sample(0), first_own, preferred_element_type=f32) + jnp.dot(
        by_sample(half), first_other, preferred_element_type=f32
    )
    sig_one = sigmoid(pre_one)
    hidden_one = (pre_one * sig_one).astype(bf16)
    pre_two = jnp.dot(hidden_one, second, preferred_element_type=f32)
    sig_two = sigmoid(pre_two)
    hidden_two = (pre_two * sig_two).astype(bf16).astype(f32)
    head = head_ref[...].astype(f32)
    logit = jnp.sum(hidden_two * head, axis=1, keepdims=True)
    label = jnp.broadcast_to(label_row, (128, samples)).T[:, 0:1]
    error = sigmoid(logit) - label
    grad_two = (error * head * (sig_two * (1.0 + pre_two * (1.0 - sig_two)))).astype(bf16)
    back = lax.dot_general(grad_two, second, nt_dims, preferred_element_type=f32)
    grad_one = (back * (sig_one * (1.0 + pre_one * (1.0 - sig_one)))).astype(bf16)

    def by_column(first):
        spread = lax.dot_general(first, grad_one, nt_dims, preferred_element_type=f32).astype(bf16)
        return jnp.concatenate(
            [spread[slot * half : (slot + 1) * half] for slot in range(slots)], axis=1
        )

    grad_input = jnp.concatenate([by_column(first_own), by_column(first_other)], axis=0)
    return lax.dot_general(grad_input, counts, nt_dims, preferred_element_type=f32)


def copies(pairs, sems):
    started = []
    for at, (source, target) in enumerate(pairs):
        copy = pltpu.make_async_copy(source, target, sems.at[at])
        copy.start()
        started.append(copy)
    return started


def lead_kernel(out_ref):
    out_ref[...] = jnp.zeros_like(out_ref)


def pick_blocks(slab_ref, blocks_ref, step, first):
    half, rows = slab_ref.shape[1:]
    tables = []
    for i in range(first, blocks_ref.shape[1]):
        chosen = jnp.broadcast_to(blocks_ref[step : step + 1, i : i + 1].astype(f32), (half, rows))
        chosen = chosen.astype(bf16)
        table = slab_ref[0]
        for block in range(1, slab_ref.shape[0]):
            table = jnp.where(chosen == jnp.asarray(block, bf16), slab_ref[block], table)
        tables.append(table)
    return jnp.concatenate(tables, axis=1)


def open_kernel(shared, lead_ref, ids_ref, labels_ref, linear_at, square_at, serve_at, pack_ref):
    steps, slots, picks, _ = ids_ref.shape
    owned, half, rows = linear_at.shape
    last = steps - 1
    pack_ref[0:owned] = linear_at[...].astype(bf16)
    pack_ref[owned : 2 * owned] = square_at[...].astype(bf16)
    pack_ref[2 * owned : 3 * owned] = serve_at[...]
    if shared:
        core = lax.axis_index("mp")
        lanes = pl.ds(pl.multiple_of(core * rows, rows), rows)
        label_rows = labels_ref[:, lanes]
        at = 3 * owned
        per = half // picks
        for part in range(slots // per):
            ids = jnp.concatenate(
                [ids_ref[last, part * per + i, :, lanes].astype(f32) for i in range(per)], axis=0
            )
            upper = jnp.floor(ids / rows)
            pack_ref[at + part] = upper.astype(bf16)
            pack_ref[at + slots // per + part] = (ids - upper * rows).astype(bf16)
        row = label_rows[last : last + 1]
        first = row.astype(bf16)
        rest = row - first.astype(f32)
        second = rest.astype(bf16)
        third = (rest - second.astype(f32)).astype(bf16)
        which = lax.broadcasted_iota(jnp.int32, (half, rows), 0)
        parts = [jnp.broadcast_to(p.astype(f32), (half, rows)) for p in (first, second, third)]
        pack_ref[at + 2 * (slots // per)] = jnp.where(
            which == 0, parts[0], jnp.where(which == 1, parts[1], parts[2])
        ).astype(bf16)


def first_step_kernel(
    samples,
    blocks_ref,
    ids_ref,
    labels_ref,
    slab_own,
    slab_other,
    w1_own,
    w1_other,
    w2_ref,
    head_ref,
    share_ref,
    rest_own,
    rest_other,
    counts_ref,
):
    active = blocks_ref.shape[1]
    half, rows = slab_other.shape[1:]
    slots = ids_ref.shape[1]
    fresh = active // 2
    core = lax.axis_index("mp")
    lanes = pl.ds(pl.multiple_of(core * samples, samples), samples)
    for slot in range(slots):
        ids = ids_ref[0, slot, :, lanes].astype(f32)
        fill_counts(counts_ref, ids, slot * samples, active, rows)
    tables = [pick_blocks(slab, blocks_ref, 0, 0) for slab in (slab_own, slab_other)]
    grad = step_body(
        jnp.concatenate(tables, axis=0),
        counts_ref[...],
        labels_ref[0:1, lanes],
        w1_own,
        w1_other,
        w2_ref,
        head_ref,
        slots,
    )
    for i in range(active):
        part = grad[:, i * rows : (i + 1) * rows].astype(bf16)
        if i < fresh:
            rest_own[i] = part[:half]
            rest_other[i] = part[half:]
        else:
            share_ref[i - fresh] = part[:half]
            share_ref[active - fresh + i - fresh] = part[half:]


def side_kernel(picks, samples, active, ids_ref, labels_ref, req_ref, *refs):
    packs = refs[:-3]
    counts_ref, labels_out, wanted_ref = refs[-3:]
    steps, slots = ids_ref.shape[:2]
    rows = counts_ref.shape[0] // active
    total = counts_ref.shape[1] // slots
    last = steps - 1
    core = lax.axis_index("mp")
    lanes = pl.ds(pl.multiple_of(core * samples, samples), samples)
    for slot in range(slots):
        fill_counts(counts_ref, ids_ref[last, slot, :, lanes].astype(f32), slot * total, active, rows)
    labels_out[0:1, 0:samples] = labels_ref[last : last + 1, lanes]
    for k, pack in enumerate(packs):
        half = pack.shape[1]
        per = half // picks
        at = pack.shape[0] - 1 - 2 * (slots // per)
        for part in range(slots // per):
            ids = pack[at + part].astype(f32) * rows + pack[at + slots // per + part].astype(f32)
            for i in range(per):
                fill_counts(
                    counts_ref,
                    ids[i * picks : (i + 1) * picks],
                    (part * per + i) * total + (k + 1) * samples,
                    active,
                    rows,
                )
        parts = pack[pack.shape[0] - 1].astype(f32)
        labels_out[0:1, (k + 1) * samples : (k + 2) * samples] = (
            parts[0:1] + parts[1:2] + parts[2:3]
        )
    requests = req_ref.shape[0]
    lanes_ids = jnp.concatenate([req_ref[i] for i in range(requests)], axis=1).astype(f32)
    fill_counts(wanted_ref, lanes_ids, 0, wanted_ref.shape[0] // rows, rows)


def state_kernel(owners, packs_count, *refs):
    blocks_ref, layout_ref, linear_ref, square_ref, serve_ref, slab_own = refs[:6]
    packs = refs[6 : 6 + packs_count]
    linear_out, square_out, weight_out, table_out, where_out, mine_out = refs[6 + packs_count :]
    active = blocks_ref.shape[1]
    owned, half, rows = linear_ref.shape
    fresh = active // 2
    touched = active + fresh
    me = lax.axis_index("dp")
    for k in range(owners):
        if packs_count == 1:
            table_out[k * owned : (k + 1) * owned] = packs[0][k, 2 * owned : 3 * owned]
        elif k == 0:
            table_out[pl.ds(me * owned, owned)] = serve_ref[...]
        else:
            table_out[pl.ds((me ^ k) * owned, owned)] = packs[k - 1][2 * owned : 3 * owned]
    for i in range(touched):
        if i < active - fresh:
            step, at = 0, fresh + i
        elif i < active:
            step, at = 0, i - (active - fresh)
        else:
            step, at = 1, i - fresh
        block = jnp.broadcast_to(blocks_ref[step : step + 1, at : at + 1], (8, rows))
        wide = jnp.broadcast_to(block[0:1], (half, rows))
        linear = jnp.zeros((half, rows), f32)
        square = jnp.zeros((half, rows), f32)
        weight = jnp.zeros((half, rows), f32)
        for k in range(owners):
            for place in range(owned):
                if packs_count == 1:
                    hit = (wide == k * owned + place) & (k != me)
                    old = packs[0][k, place].astype(f32), packs[0][k, owned + place].astype(f32)
                else:
                    hit = wide == (me ^ k) * owned + place
                    if k == 0:
                        old = linear_ref[place], square_ref[place]
                    else:
                        old = (
                            packs[k - 1][place].astype(f32),
                            packs[k - 1][owned + place].astype(f32),
                        )
                linear = jnp.where(hit, old[0], linear)
                square = jnp.where(hit, old[1], square)
                here = k * owned + place
                weight = jnp.where(wide == here, slab_own[here].astype(f32), weight)
        if packs_count == 1:
            for place in range(owned):
                hit = wide == me * owned + place
                linear = jnp.where(hit, linear_ref[place], linear)
                square = jnp.where(hit, square_ref[place], square)
        linear_out[i], square_out[i], weight_out[i] = linear, square, weight
        owner = block // owned
        place = block % owned
        turn = (owner + place) % owners
        home = jnp.zeros_like(block)
        for q in range(owners):
            home = jnp.where(turn == q, layout_ref[0:1, q : q + 1], home)
        where_out[i] = home * owned + place
        mine_out[i] = jnp.where(owner == me, place, -1)


def share_update(linear_ref, square_ref, weight_ref, sums, count, low):
    parts = []
    for i in range(count):
        gradient = tree_sum([part[low + i].astype(f32) for part in sums])
        parts.append(ftrl_update(linear_ref[i], square_ref[i], gradient, weight_ref[i]))
    return parts


def second_step_kernel(slots, sums_count, blocks_ref, counts_ref, labels_ref, *refs):
    sums = refs[:sums_count]
    linear_own, square_own, weight_own, other_state, slab_own, slab_other = refs[sums_count:][:6]
    rest_own, rest_other, w1_own, w1_other, w2_ref, head_ref = refs[sums_count + 6 :][:6]
    out_own, out_other, new_out, linear_out, square_out = refs[sums_count + 12 :]
    active = blocks_ref.shape[1]
    half, rows = slab_own.shape[1:]
    fresh = active // 2
    shared = active - fresh
    last = blocks_ref.shape[0] - 1
    own = share_update(linear_own, square_own, weight_own, sums, shared, 0)
    other = share_update(
        other_state.at[0:shared],
        other_state.at[shared : 2 * shared],
        other_state.at[2 * shared : 3 * shared],
        sums,
        shared,
        shared,
    )
    for i in range(shared):
        linear_out[i], square_out[i] = own[i][:2]
        new_out[i] = own[i][2].astype(bf16).astype(f32)

    def table(updated, slab):
        return jnp.concatenate(
            [part[2].astype(bf16) for part in updated]
            + [pick_blocks(slab, blocks_ref, last, shared)],
            axis=1,
        )

    grad = step_body(
        jnp.concatenate([table(own, slab_own), table(other, slab_other)], axis=0),
        counts_ref[...],
        labels_ref[0:1],
        w1_own,
        w1_other,
        w2_ref,
        head_ref,
        slots,
    )
    for i in range(fresh):
        out_own[shared + i] = rest_own[i]
        out_other[shared + i] = rest_other[i]
    for i in range(active):
        part = grad[:, i * rows : (i + 1) * rows].astype(bf16)
        at = i if i < shared else fresh + i
        out_own[at] = part[:half]
        out_other[at] = part[half:]


def finish_kernel(sums_count, *refs):
    linear_old, square_old, weight_old, table_ref, where_ref, mine_ref = refs[:6]
    new_ref, linear_mid, square_mid, counts_ref, w1_own = refs[6:11]
    linear_in, square_in, serve_in = refs[11:14]
    sums = refs[14 : 14 + sums_count]
    linear_hbm, square_hbm, serve_hbm, partial_out = refs[14 + sums_count :][:4]
    linear_at, square_at, serve_at, sems = refs[14 + sums_count + 4 :]
    touched, half, rows = linear_old.shape
    owned = linear_in.shape[0]
    shared = new_ref.shape[0]
    positions = table_ref.shape[0]
    me = lax.axis_index("dp")
    weights, linears, squares = [], [], []
    for i in range(touched):
        gradient = tree_sum([part[i].astype(f32) for part in sums])
        if i < shared:
            old = linear_mid[i], square_mid[i], new_ref[i]
        else:
            old = linear_old[i], square_old[i], weight_old[i]
        linear, square, weight = ftrl_update(old[0], old[1], gradient, old[2])
        linears.append(linear)
        squares.append(square)
        weights.append(weight)

    def wide(ref, i):
        return jnp.broadcast_to(ref[i][0:1], (half, rows))

    home = [wide(mine_ref, i) for i in range(touched)]
    goal = [wide(where_ref, i) for i in range(touched)]
    for place in range(owned):
        linear, square = linear_in[place], square_in[place]
        serve = serve_in[place].astype(f32)
        for i in range(touched):
            hit = home[i] == place
            linear = jnp.where(hit, linears[i], linear)
            square = jnp.where(hit, squares[i], square)
            serve = jnp.where(goal[i] == me * owned + place, weights[i], serve)
        linear_at[place] = linear
        square_at[place] = square
        serve_at[place] = serve.astype(bf16)
    started = copies(
        [(linear_at, linear_hbm), (square_at, square_hbm), (serve_at, serve_hbm)], sems
    )
    tables = []
    for position in range(positions):
        table = table_ref[position].astype(f32)
        for i in range(touched):
            table = jnp.where(goal[i] == position, weights[i], table)
        tables.append(table.astype(bf16))
    pooled = jnp.dot(jnp.concatenate(tables, axis=1), counts_ref[...], preferred_element_type=f32)
    units = w1_own.shape[1]
    slots = w1_own.shape[0] // half
    requests = counts_ref.shape[1] // slots
    stacked = jnp.concatenate([pooled] * slots, axis=0)
    wanted = lax.broadcasted_iota(jnp.int32, stacked.shape, 0) // half
    present = lax.broadcasted_iota(jnp.int32, stacked.shape, 1) % slots
    stacked = jnp.where(wanted == present, stacked, 0.0)
    product = jnp.dot(stacked.T.astype(bf16), w1_own[...], preferred_element_type=f32)
    partial_out[...] = jnp.sum(product.reshape(requests, slots, units), axis=1)
    for copy in started:
        copy.wait()


def score_kernel(own_ref, other_ref, w2_ref, head_ref, out_ref):
    pre_one = own_ref[...] + other_ref[...]
    hidden_one = (pre_one * sigmoid(pre_one)).astype(bf16)
    pre_two = jnp.dot(hidden_one, w2_ref[...], preferred_element_type=f32)
    hidden_two = (pre_two * sigmoid(pre_two)).astype(bf16).astype(f32)
    logit = jnp.sum(hidden_two * head_ref[...].astype(f32), axis=1, keepdims=True)
    requests = logit.shape[0]
    out_ref[...] = jnp.broadcast_to(logit, (requests, 128)).T[0:1, :requests]


def swap(value, axes, sizes, bits):
    shape = tuple(sizes[a] for a in axes)
    count = 1
    for size in shape:
        count *= size
    pairs = []
    for index in range(count):
        rest, coords = index, []
        for size in reversed(shape):
            coords.append(rest % size)
            rest //= size
        coords = coords[::-1]
        target = 0
        for coord, bit, size in zip(coords, bits, shape):
            target = target * size + (coord ^ bit)
        pairs.append((index, target))
    return lax.ppermute(value, axes, pairs)


def add(parts):
    return tree_sum([p.astype(f32) for p in parts]).astype(bf16)


def reduce_rest(parts, sizes, first_bit):
    replicas, owners = sizes["replica"], sizes["dp"]
    bit = 2
    while bit < replicas:
        total = add(parts)
        parts = [total, swap(total, ("replica",), sizes, (bit,))]
        bit *= 2
    bit = first_bit
    while bit < owners:
        total = add(parts)
        steps = [k * bit for k in range(1, 4) if k * bit < owners]
        parts = [total] + [swap(total, ("dp",), sizes, (k,)) for k in steps]
        bit *= 4
    return parts


def exchange_whole(both, sizes):
    count = both.shape[0] // 2

    def turned(value):
        return jnp.concatenate([value[count:], value[:count]], axis=0)

    parts = [both]
    if sizes["replica"] > 1:
        parts.append(swap(both, ("replica", "mp"), sizes, (1, 0)))
    parts.append(turned(swap(both, ("replica", "mp"), sizes, (0, 1))))
    if sizes["replica"] > 1:
        parts.append(turned(swap(both, ("replica", "mp"), sizes, (1, 1))))
    return parts


def reduce_halves(own, other, sizes, first_bit):
    parts = [own]
    if sizes["replica"] > 1:
        parts.append(swap(own, ("replica", "mp"), sizes, (1, 0)))
    parts.append(swap(other, ("replica", "mp"), sizes, (0, 1)))
    if sizes["replica"] > 1:
        parts.append(swap(other, ("replica", "mp"), sizes, (1, 1)))
    return reduce_rest(parts, sizes, first_bit)


def local(
    sizes,
    hot_slab,
    linear_state,
    square_state,
    serve_table,
    first_weight,
    second_weight,
    out_weight,
    step_blocks,
    feature_ids,
    click_labels,
    serve_layout,
    request_ids,
):
    owners = sizes["dp"]
    owned, half, rows = linear_state.shape
    steps, active = step_blocks.shape
    fresh = active // 2
    kept = active - fresh
    touched = active + fresh
    samples = feature_ids.shape[1] // sizes["mp"]
    slots, picks = feature_ids.shape[2:]
    units = first_weight.shape[2]
    ids = jnp.transpose(feature_ids, (0, 2, 3, 1))
    req = jnp.transpose(request_ids[0], (0, 2, 1))
    requests = req.shape[0]
    positions = owners * owned
    w1_own = first_weight.reshape(-1, units)
    w1_other = swap(w1_own, ("mp",), sizes, (1,))
    slab_other = swap(hot_slab, ("mp",), sizes, (1,))
    head = out_weight.reshape(1, -1)
    serve_own = serve_table[0]
    direct = owners == 4
    shared = share_owners and direct and samples == rows
    members = owners if shared else 1

    def struct(*shape, dtype=bf16):
        return jax.ShapeDtypeStruct(shape, dtype)

    extra = 2 * (slots * picks // half) + 1 if shared else 0
    lead = kernel_call(lead_kernel, struct(8, 128, dtype=f32), [], micros=20.0)()
    pack = kernel_call(
        functools.partial(open_kernel, shared),
        struct(3 * owned + extra, half, rows),
        [VMEM] * 6,
    )(lead, ids, click_labels, linear_state, square_state, serve_own)
    if direct:
        packs = [swap(pack, ("dp",), sizes, (k,)) for k in range(1, owners)]
    else:
        packs = [lax.all_gather(pack, "dp", axis=0, tiled=False)]

    share, rest_own, rest_other = kernel_call(
        functools.partial(first_step_kernel, samples),
        (struct(2 * kept, half, rows), struct(fresh, half, rows), struct(fresh, half, rows)),
        [VMEM] * 9,
        [pltpu.VMEM((active * rows, slots * samples), bf16)],
    )(
        step_blocks,
        ids,
        click_labels,
        hot_slab,
        slab_other,
        w1_own,
        w1_other,
        second_weight,
        head,
    )
    parts = exchange_whole(share, sizes)
    late_ids, late_labels = lax.optimization_barrier((parts[2], ids, click_labels))[1:]
    counts, labels, wanted = kernel_call(
        functools.partial(side_kernel, picks, samples, active),
        (
            struct(active * rows, slots * members * samples),
            struct(1, members * samples, dtype=f32),
            struct(positions * rows, requests * slots),
        ),
        [VMEM] * (3 + (len(packs) if shared else 0)),
    )(late_ids, late_labels, req, *(packs if shared else []))

    packs = lax.optimization_barrier((share, *packs))[1:]
    linear_old, square_old, weight_old, table, where, mine = kernel_call(
        functools.partial(state_kernel, owners, len(packs)),
        (
            struct(touched, half, rows, dtype=f32),
            struct(touched, half, rows, dtype=f32),
            struct(touched, half, rows, dtype=f32),
            struct(positions, half, rows),
            struct(touched, 8, rows, dtype=jnp.int32),
            struct(touched, 8, rows, dtype=jnp.int32),
        ),
        [VMEM] * (6 + len(packs)),
        micros=1.0,
    )(step_blocks, serve_layout, linear_state, square_state, serve_own, hot_slab, *packs)
    tied = lax.optimization_barrier((counts, linear_old, square_old, weight_old, *parts))
    counts, linear_old, square_old, weight_old = tied[:4]
    first_sum = add(tied[4:])
    sums = reduce_rest([first_sum], sizes, 1)
    other_state = swap(
        jnp.concatenate([linear_old[:kept], square_old[:kept], weight_old[:kept]], axis=0),
        ("mp",),
        sizes,
        (1,),
    )
    grad_own, grad_other, new_own, linear_mid, square_mid = kernel_call(
        functools.partial(second_step_kernel, slots, len(sums)),
        (
            struct(touched, half, rows),
            struct(touched, half, rows),
            struct(kept, half, rows, dtype=f32),
            struct(kept, half, rows, dtype=f32),
            struct(kept, half, rows, dtype=f32),
        ),
        [VMEM] * (3 + len(sums) + 12),
    )(
        step_blocks,
        counts,
        labels,
        *sums,
        linear_old,
        square_old,
        weight_old,
        other_state,
        hot_slab,
        slab_other,
        rest_own,
        rest_other,
        w1_own,
        w1_other,
        second_weight,
        head,
    )
    sums = reduce_halves(grad_own, grad_other, sizes, members)
    linear_out, square_out, serve_out, partial = kernel_call(
        functools.partial(finish_kernel, len(sums)),
        (
            struct(*linear_state.shape, dtype=f32),
            struct(*square_state.shape, dtype=f32),
            struct(*serve_own.shape),
            struct(requests, units, dtype=f32),
        ),
        [VMEM] * (14 + len(sums)),
        [
            pltpu.VMEM(linear_state.shape, f32),
            pltpu.VMEM(square_state.shape, f32),
            pltpu.VMEM(serve_own.shape, bf16),
            pltpu.SemaphoreType.DMA((3,)),
        ],
        (HBM, HBM, HBM, VMEM),
    )(
        linear_old,
        square_old,
        weight_old,
        table,
        where,
        mine,
        new_own,
        linear_mid,
        square_mid,
        wanted,
        w1_own,
        linear_state,
        square_state,
        serve_own,
        *sums,
    )
    partial_other = swap(partial, ("mp",), sizes, (1,))
    scores = kernel_call(score_kernel, struct(1, requests, dtype=f32), [VMEM] * 4)(
        partial, partial_other, second_weight, head
    )
    return linear_out, square_out, serve_out[None], scores


def solution(mesh):
    sizes = dict(mesh.shape)
    placed = (
        P(None, "mp", None),
        P("dp", "mp", None),
        P("dp", "mp", None),
        P("replica", "dp", "mp", None),
        P(None, "mp", None),
        P(),
        P(),
        P("groups", None),
        P(None, ("groups", "dp", "replica"), None, None),
        P(None, ("groups", "dp", "replica")),
        P("replica", None),
        P("replica", ("groups", "dp"), None, None),
    )
    return jax.shard_map(
        functools.partial(local, sizes),
        mesh=mesh,
        in_specs=placed,
        out_specs=(
            P(("groups", "dp"), "mp", None),
            P(("groups", "dp"), "mp", None),
            P(("groups", "replica"), "dp", "mp", None),
            P("replica", ("groups", "dp")),
        ),
        check_vma=False,
    )
```

```python
import functools

import jax
import jax.numpy as jnp
from jax import lax
from jax.experimental import pallas as pl
from jax.experimental.pallas import tpu as pltpu
from jax.sharding import PartitionSpec as P

step_alpha = 0.5
step_beta = 1.0
sparse_penalty = 0.1
ridge_penalty = 0.05
f32 = jnp.float32
bf16 = jnp.bfloat16
VMEM = pl.BlockSpec(memory_space=pltpu.VMEM)
HBM = pl.BlockSpec(memory_space=pltpu.HBM)
nt_dims = (((1,), (1,)), ((), ()))


def kernel_call(body, out_shape, in_specs, scratch=(), out_specs=None, micros=1.0, limit=32):
    return pl.pallas_call(
        body,
        out_shape=out_shape,
        in_specs=in_specs,
        out_specs=jax.tree.map(lambda _: VMEM, out_shape) if out_specs is None else out_specs,
        scratch_shapes=list(scratch),
        compiler_params=pltpu.CompilerParams(vmem_limit_bytes=limit * 1024 * 1024),
        cost_estimate=pl.CostEstimate(
            flops=int(micros * 1e9), bytes_accessed=int(micros * 1e6), transcendentals=0
        ),
    )


def sigmoid(v):
    return 0.5 * jnp.tanh(0.5 * v) + 0.5


def ftrl_update(linear, square, gradient, current):
    grown = square + gradient * gradient
    root = jnp.sqrt(grown)
    sigma_term = (root - jnp.sqrt(square)) / step_alpha
    linear_next = linear + gradient - sigma_term * current
    shrunk = linear_next - jnp.clip(linear_next, -sparse_penalty, sparse_penalty)
    weights = -shrunk / ((step_beta + root) / step_alpha + ridge_penalty)
    return linear_next, grown, weights


def fill_counts(counts_ref, ids, column, blocks, rows):
    picks, lanes = ids.shape
    tiles = rows // 16
    level = lax.broadcasted_iota(jnp.int32, (tiles, 16, lanes), 1) + 16 * lax.broadcasted_iota(
        jnp.int32, (tiles, 16, lanes), 0
    )
    level = level.astype(f32).astype(bf16)
    wide = [jnp.broadcast_to(ids[pick : pick + 1], (16, lanes)) for pick in range(picks)]
    times = []
    for pick in range(picks):
        total = jnp.ones((16, lanes), f32)
        for later in range(pick + 1, picks):
            total = total + jnp.where(wide[later] == wide[pick], 1.0, 0.0)
        times.append(total.astype(bf16)[None])
    zero = jnp.zeros((), bf16)
    for block in range(blocks):
        filled = None
        for pick in reversed(range(picks)):
            place = (wide[pick] - float(block * rows)).astype(bf16)[None]
            filled = jnp.where(level == place, times[pick], zero if filled is None else filled)
        counts_ref[block * rows : (block + 1) * rows, column : column + lanes] = filled.reshape(
            rows, lanes
        )


def tree_sum(parts):
    parts = list(parts)
    while len(parts) > 1:
        parts = [
            parts[i] + parts[i + 1] if i + 1 < len(parts) else parts[i]
            for i in range(0, len(parts), 2)
        ]
    return parts[0]


def copies(pairs, sems):
    started = []
    for at, (source, target) in enumerate(pairs):
        copy = pltpu.make_async_copy(source, target, sems.at[at])
        copy.start()
        started.append(copy)
    return started


def lead_kernel(out_ref):
    out_ref[...] = jnp.zeros_like(out_ref)


def pick_blocks(slab_ref, blocks_ref, step, first):
    half, rows = slab_ref.shape[1:]
    tables = []
    for i in range(first, blocks_ref.shape[1]):
        chosen = jnp.broadcast_to(blocks_ref[step : step + 1, i : i + 1].astype(f32), (half, rows))
        chosen = chosen.astype(bf16)
        table = slab_ref[0]
        for block in range(1, slab_ref.shape[0]):
            table = jnp.where(chosen == jnp.asarray(block, bf16), slab_ref[block], table)
        tables.append(table)
    return jnp.concatenate(tables, axis=1)


def lead_kernel(out_ref):
    out_ref[...] = jnp.zeros_like(out_ref)


def open_kernel(lead_ref, ids_ref, labels_ref, linear_ref, square_ref, serve_ref, out_ref, pack_ref):
    owned = linear_ref.shape[0]
    pack_ref[0:owned] = linear_ref[...].astype(bf16)
    pack_ref[owned : 2 * owned] = square_ref[...].astype(bf16)
    pack_ref[2 * owned : 3 * owned] = serve_ref[...]
    steps, slots, picks, _ = ids_ref.shape
    samples = out_ref.shape[1]
    core = lax.axis_index("mp")
    lanes = pl.ds(pl.multiple_of(core * samples, samples), samples)
    for step in range(steps):
        for slot in range(slots):
            low = (step * slots + slot) * picks
            out_ref[low : low + picks] = ids_ref[step, slot, :, lanes].astype(f32)
    low = steps * slots * picks
    out_ref[low:] = jnp.zeros((out_ref.shape[0] - low, samples), f32)
    out_ref[low : low + steps] = labels_ref[:, lanes]


def fill_step(counts_ref, note_ref, step, slots, picks, active, rows):
    samples = note_ref.shape[1]
    for slot in range(slots):
        low = (step * slots + slot) * picks
        fill_counts(counts_ref, note_ref[low : low + picks], slot * samples, active, rows)


def by_sample(pooled, slots):
    half = pooled.shape[0] // 2
    samples = pooled.shape[1] // slots
    out = []
    for low in (0, half):
        stacked = jnp.concatenate(
            [
                pooled[low : low + half, slot * samples : (slot + 1) * samples]
                for slot in range(slots)
            ],
            axis=0,
        )
        out.append(stacked.T.astype(bf16))
    return out


def network(inputs, label_rows, counts, w1_own, w1_other, w2_ref, head_ref, slots):
    half = w1_own.shape[0] // slots
    first_own, first_other, second = w1_own[...], w1_other[...], w2_ref[...]
    inputs_own = jnp.concatenate([part[0] for part in inputs], axis=0)
    inputs_other = jnp.concatenate([part[1] for part in inputs], axis=0)
    pre_one = jnp.dot(inputs_own, first_own, preferred_element_type=f32) + jnp.dot(
        inputs_other, first_other, preferred_element_type=f32
    )
    sig_one = sigmoid(pre_one)
    hidden_one = (pre_one * sig_one).astype(bf16)
    pre_two = jnp.dot(hidden_one, second, preferred_element_type=f32)
    sig_two = sigmoid(pre_two)
    hidden_two = (pre_two * sig_two).astype(bf16).astype(f32)
    head = head_ref[...].astype(f32)
    logit = jnp.sum(hidden_two * head, axis=1, keepdims=True)
    label = jnp.concatenate(
        [jnp.broadcast_to(row, (128, row.shape[1])).T[:, 0:1] for row in label_rows], axis=0
    )
    error = sigmoid(logit) - label
    grad_two = (error * head * (sig_two * (1.0 + pre_two * (1.0 - sig_two)))).astype(bf16)
    back = lax.dot_general(grad_two, second, nt_dims, preferred_element_type=f32)
    grad_one = (back * (sig_one * (1.0 + pre_one * (1.0 - sig_one)))).astype(bf16)
    spread = [
        lax.dot_general(first, grad_one, nt_dims, preferred_element_type=f32).astype(bf16)
        for first in (first_own, first_other)
    ]
    samples = spread[0].shape[1] // len(counts)
    total = None
    for group, group_counts in enumerate(counts):
        lanes = slice(group * samples, (group + 1) * samples)
        grad_input = jnp.concatenate(
            [
                jnp.concatenate(
                    [part[slot * half : (slot + 1) * half, lanes] for slot in range(slots)], axis=1
                )
                for part in spread
            ],
            axis=0,
        )
        grad = lax.dot_general(grad_input, group_counts, nt_dims, preferred_element_type=f32)
        grad = grad.astype(bf16).astype(f32)
        total = grad if total is None else total + grad
    return total


def first_step_kernel(slots, picks, groups, blocks_ref, *refs):
    notes = refs[:groups]
    slab_own, slab_other, w1_own, w1_other, w2_ref, head_ref = refs[groups : groups + 6]
    share_ref, rest_own = refs[groups + 6 : groups + 8]
    counts_refs = refs[groups + 8 :]
    active = blocks_ref.shape[1]
    half, rows = slab_other.shape[1:]
    fresh = active // 2
    kept = active - fresh
    labels = notes[0].shape[0] // 8 * 8 - 8
    table = jnp.concatenate(
        [pick_blocks(slab, blocks_ref, 0, 0) for slab in (slab_own, slab_other)], axis=0
    )
    inputs = []
    for note, counts_ref in zip(notes, counts_refs):
        fill_step(counts_ref, note, 0, slots, picks, active, rows)
        pooled = jnp.dot(table, counts_ref[...], preferred_element_type=f32)
        inputs.append(by_sample(pooled, slots))
    grad = network(
        inputs,
        [note[labels : labels + 1] for note in notes],
        [ref[...] for ref in counts_refs],
        w1_own,
        w1_other,
        w2_ref,
        head_ref,
        slots,
    )
    for i in range(active):
        part = grad[:, i * rows : (i + 1) * rows].astype(bf16)
        if i < fresh:
            rest_own[i] = part[:half]
            share_ref[2 * kept + i] = part[half:]
        else:
            share_ref[i - fresh] = part[:half]
            share_ref[kept + i - fresh] = part[half:]


def side_kernel(slots, picks, active, groups, rows, *refs):
    notes = refs[:groups]
    req_ref = refs[groups]
    counts_refs = refs[groups + 1 : 2 * groups + 1]
    wanted_ref = refs[2 * groups + 1]
    for note, counts_ref in zip(notes, counts_refs):
        fill_step(counts_ref, note, 1, slots, picks, active, rows)
    requests = req_ref.shape[0]
    lanes_ids = jnp.concatenate([req_ref[i] for i in range(requests)], axis=1).astype(f32)
    fill_counts(wanted_ref, lanes_ids, 0, wanted_ref.shape[0] // rows, rows)


def join_kernel(turned, *refs):
    *sums, out_ref = refs
    if turned:
        first, second, rest = sums
        half = (first.shape[0] - rest.shape[0]) // 2
        low = first[0:half].astype(f32) + second[half : 2 * half].astype(f32)
        high = first[half : 2 * half].astype(f32) + second[0:half].astype(f32)
        out_ref[0:half] = low.astype(bf16)
        out_ref[half : 2 * half] = high.astype(bf16)
        rest = rest[...].astype(f32) + second[2 * half :].astype(f32)
        out_ref[2 * half :] = rest.astype(bf16)
    else:
        out_ref[...] = tree_sum([part[...].astype(f32) for part in sums]).astype(bf16)


def tree_sum(parts):
    parts = list(parts)
    while len(parts) > 1:
        parts = [
            parts[i] + parts[i + 1] if i + 1 < len(parts) else parts[i]
            for i in range(0, len(parts), 2)
        ]
    return parts[0]


def old_state(block, me, owners, linear_ref, square_ref, slab_own, packs):
    owned, half, rows = linear_ref.shape
    linear = jnp.zeros((half, rows), f32)
    square = jnp.zeros((half, rows), f32)
    weight = jnp.zeros((half, rows), f32)
    gathered = len(packs) == 1
    for k in range(owners):
        for place in range(owned):
            here = k * owned + place
            weight = jnp.where(block == here, slab_own[here].astype(f32), weight)
            if gathered:
                hit = block == here
                old = packs[0][k, place].astype(f32), packs[0][k, owned + place].astype(f32)
            else:
                hit = block == (me ^ k) * owned + place
                if k == 0:
                    old = linear_ref[place], square_ref[place]
                else:
                    pack = packs[k - 1]
                    old = (
                        pack[place].astype(f32),
                        pack[owned + place].astype(f32),
                    )
            linear = jnp.where(hit, old[0], linear)
            square = jnp.where(hit, old[1], square)
    if gathered:
        for place in range(owned):
            hit = block == me * owned + place
            linear = jnp.where(hit, linear_ref[place], linear)
            square = jnp.where(hit, square_ref[place], square)
    return linear, square, weight


def state_kernel(owners, blocks_ref, layout_ref, linear_ref, square_ref, slab_own, *refs):
    packs = refs[:-6]
    linear_out, square_out, weight_out, where_out, mine_out, cross_out = refs[-6:]
    active = blocks_ref.shape[1]
    owned, half, rows = linear_ref.shape
    fresh = active // 2
    kept = active - fresh
    me = lax.axis_index("dp")
    for i in range(active + fresh):
        step, at = (1, i) if i < active else (0, i - active)
        block = jnp.broadcast_to(blocks_ref[step : step + 1, at : at + 1], (8, rows))
        wide = jnp.broadcast_to(block[0:1], (half, rows))
        old = old_state(wide, me, owners, linear_ref, square_ref, slab_own, packs)
        linear_out[i], square_out[i], weight_out[i] = old
        if i < kept:
            cross_out[i], cross_out[kept + i], cross_out[2 * kept + i] = old
        owner = block // owned
        place = block % owned
        turn = (owner + place) % owners
        home = jnp.zeros_like(block)
        for q in range(owners):
            home = jnp.where(turn == q, layout_ref[0:1, q : q + 1], home)
        where_out[i] = home * owned + place
        mine_out[i] = jnp.where(owner == me, place, -1)


def second_step_kernel(slots, picks, groups, steps, sums_count, blocks_ref, *refs):
    counts_refs = refs[:groups]
    notes = refs[groups : 2 * groups]
    sums = refs[2 * groups : 2 * groups + sums_count]
    refs = refs[2 * groups + sums_count :]
    linear_own, square_own, weight_own, cross, slab_own, slab_other = refs[:6]
    w1_own, w1_other, w2_ref, head_ref = refs[6:10]
    out_own, out_other, new_out, linear_out, square_out = refs[10:]
    active = blocks_ref.shape[1]
    half, rows = slab_own.shape[1:]
    fresh = active // 2
    kept = active - fresh
    labels = notes[0].shape[0] // 8 * 8 - 8 + 1

    new_own, new_other = [], []
    for i in range(kept):
        gradient = tree_sum([part[i].astype(f32) for part in sums])
        linear, square, weights = ftrl_update(linear_own[i], square_own[i], gradient, weight_own[i])
        linear_out[i] = linear
        square_out[i] = square
        new_own.append(weights.astype(bf16))
        new_out[i] = new_own[i]
        gradient = tree_sum([part[kept + i].astype(f32) for part in sums])
        weights = ftrl_update(cross[i], cross[kept + i], gradient, cross[2 * kept + i])[2]
        new_other.append(weights.astype(bf16))

    def table(new, slab):
        return jnp.concatenate(new + [pick_blocks(slab, blocks_ref, steps - 1, kept)], axis=1)

    full = jnp.concatenate([table(new_own, slab_own), table(new_other, slab_other)], axis=0)
    counts = [ref[...] for ref in counts_refs]
    inputs = [
        by_sample(jnp.dot(full, group, preferred_element_type=f32), slots) for group in counts
    ]
    grad = network(
        inputs,
        [note[labels : labels + 1] for note in notes],
        counts,
        w1_own,
        w1_other,
        w2_ref,
        head_ref,
        slots,
    )
    for i in range(active):
        part = grad[:, i * rows : (i + 1) * rows].astype(bf16)
        out_own[i] = part[:half]
        out_other[i] = part[half:]


def finish_kernel(owners, sums_count, early_count, *refs):
    linear_old, square_old, weight_old, where_ref, mine_ref = refs[:5]
    new_ref, linear_mid, square_mid, counts_ref, w1_own = refs[5:10]
    linear_in, square_in, serve_in = refs[10:13]
    sums = refs[13 : 13 + sums_count]
    early = refs[13 + sums_count : 13 + sums_count + early_count]
    packs = refs[13 + sums_count + early_count : -5]
    linear_at, square_at, serve_at, partial_out, table_at = refs[-5:]
    touched, _, rows = where_ref.shape
    owned, half, _ = linear_in.shape
    kept = new_ref.shape[0]
    active = sums[0].shape[0]
    positions = table_at.shape[0]
    me = lax.axis_index("dp")
    for k in range(owners):
        if len(packs) == 1:
            table_at[k * owned : (k + 1) * owned] = packs[0][k, 2 * owned : 3 * owned]
        elif k == 0:
            table_at[pl.ds(me * owned, owned)] = serve_in[...]
        else:
            table_at[pl.ds((me ^ k) * owned, owned)] = packs[k - 1][2 * owned : 3 * owned]
    weights, linears, squares = [], [], []
    for i in range(touched):
        parts = [p[i] for p in sums] if i < active else [p[2 * kept + i - active] for p in early]
        gradient = tree_sum([part.astype(f32) for part in parts])
        if i < kept:
            old = linear_mid[i], square_mid[i], new_ref[i].astype(f32)
        else:
            old = linear_old[i], square_old[i], weight_old[i]
        linear, square, weight = ftrl_update(old[0], old[1], gradient, old[2])
        linears.append(linear)
        squares.append(square)
        weights.append(weight)

    def wide(ref, i):
        return jnp.broadcast_to(ref[i][0:1], (half, rows))

    home = [wide(mine_ref, i) for i in range(touched)]
    goal = [wide(where_ref, i) for i in range(touched)]
    for place in range(owned):
        linear, square = linear_in[place], square_in[place]
        serve = serve_in[place].astype(f32)
        for i in range(touched):
            hit = home[i] == place
            linear = jnp.where(hit, linears[i], linear)
            square = jnp.where(hit, squares[i], square)
            serve = jnp.where(goal[i] == me * owned + place, weights[i], serve)
        linear_at[place] = linear
        square_at[place] = square
        serve_at[place] = serve.astype(bf16)
    tables = []
    for position in range(positions):
        table = table_at[position].astype(f32)
        for i in range(touched):
            table = jnp.where(goal[i] == position, weights[i], table)
        tables.append(table.astype(bf16))
    pooled = jnp.dot(jnp.concatenate(tables, axis=1), counts_ref[...], preferred_element_type=f32)
    units = w1_own.shape[1]
    slots = w1_own.shape[0] // half
    requests = counts_ref.shape[1] // slots
    stacked = jnp.concatenate([pooled] * slots, axis=0)
    wanted = lax.broadcasted_iota(jnp.int32, stacked.shape, 0) // half
    present = lax.broadcasted_iota(jnp.int32, stacked.shape, 1) % slots
    stacked = jnp.where(wanted == present, stacked, 0.0)
    product = jnp.dot(stacked.T.astype(bf16), w1_own[...], preferred_element_type=f32)
    partial_out[...] = jnp.sum(product.reshape(requests, slots, units), axis=1)


def write_kernel(*refs):
    count = len(refs) // 2
    for copy in copies(list(zip(refs[:count], refs[count : 2 * count])), refs[-1]):
        copy.wait()


def score_kernel(own_ref, other_ref, w2_ref, head_ref, out_ref):
    pre_one = own_ref[...] + other_ref[...]
    hidden_one = (pre_one * sigmoid(pre_one)).astype(bf16)
    pre_two = jnp.dot(hidden_one, w2_ref[...], preferred_element_type=f32)
    hidden_two = (pre_two * sigmoid(pre_two)).astype(bf16).astype(f32)
    logit = jnp.sum(hidden_two * head_ref[...].astype(f32), axis=1, keepdims=True)
    requests = logit.shape[0]
    out_ref[...] = jnp.broadcast_to(logit, (requests, 128)).T[0:1, :requests]


def swap(value, axes, sizes, bits):
    shape = tuple(sizes[a] for a in axes)
    count = 1
    for size in shape:
        count *= size
    pairs = []
    for index in range(count):
        rest, coords = index, []
        for size in reversed(shape):
            coords.append(rest % size)
            rest //= size
        coords = coords[::-1]
        target = 0
        for coord, bit, size in zip(coords, bits, shape):
            target = target * size + (coord ^ bit)
        pairs.append((index, target))
    return lax.ppermute(value, axes, pairs)


def join(parts, turned=False):
    return kernel_call(
        functools.partial(join_kernel, turned),
        jax.ShapeDtypeStruct(parts[0].shape, bf16),
        [VMEM] * len(parts),
    )(*parts)


def reduce_rest(total, sizes, groups):
    parts = [total]
    bit = groups
    while bit < sizes["replica"]:
        total = join(parts) if len(parts) > 1 else total
        parts = [total, swap(total, ("replica",), sizes, (bit,))]
        bit *= 2
    bit = 1
    while bit < sizes["dp"]:
        total = join(parts) if len(parts) > 1 else total
        steps = [k * bit for k in range(1, 4) if k * bit < sizes["dp"]]
        parts = [total] + [swap(total, ("dp",), sizes, (k,)) for k in steps]
        bit *= 4
    return parts


def local(
    sizes,
    hot_slab,
    linear_state,
    square_state,
    serve_table,
    first_weight,
    second_weight,
    out_weight,
    step_blocks,
    feature_ids,
    click_labels,
    serve_layout,
    request_ids,
):
    owners = sizes["dp"]
    owned, half, rows = linear_state.shape
    steps, active = step_blocks.shape
    fresh = active // 2
    kept = active - fresh
    touched = active + fresh
    samples = feature_ids.shape[1] // sizes["mp"]
    slots, picks = feature_ids.shape[2:]
    units = first_weight.shape[2]
    ids = jnp.transpose(feature_ids, (0, 2, 3, 1))
    req = jnp.transpose(request_ids[0], (0, 2, 1))
    requests = req.shape[0]
    positions = owners * owned
    groups = 2 if sizes["replica"] > 1 else 1
    direct = owners == 4

    def struct(*shape, dtype=bf16):
        return jax.ShapeDtypeStruct(shape, dtype)

    w1_own = first_weight.reshape(-1, units)
    w1_other = swap(w1_own, ("mp",), sizes, (1,))
    slab_other = swap(hot_slab, ("mp",), sizes, (1,))
    head = out_weight.reshape(1, -1)
    serve_own = serve_table[0]

    lead = kernel_call(lead_kernel, struct(8, 128, dtype=f32), [], micros=20.0)()
    note, pack = kernel_call(
        open_kernel,
        (struct(steps * slots * picks + 8, samples, dtype=f32), struct(3 * owned, half, rows)),
        [VMEM] * 6,
    )(lead, ids, click_labels, linear_state, square_state, serve_own)
    if direct:
        packs = [swap(pack, ("dp",), sizes, (k,)) for k in range(1, owners)]
    else:
        packs = [lax.all_gather(pack, "dp", axis=0, tiled=False)]
    notes = [note]
    if groups > 1:
        notes.append(swap(note, ("replica",), sizes, (1,)))

    counts_shape = struct(active * rows, slots * samples)
    share, rest_own = kernel_call(
        functools.partial(first_step_kernel, slots, picks, groups),
        (struct(2 * kept + fresh, half, rows), struct(fresh, half, rows)),
        [VMEM] * (7 + groups),
        [pltpu.VMEM(counts_shape.shape, bf16)] * groups,
    )(
        step_blocks,
        *notes,
        hot_slab,
        slab_other,
        w1_own,
        w1_other,
        second_weight,
        head,
    )
    share_turned = swap(share, ("mp",), sizes, (1,))
    late = lax.optimization_barrier((share, *packs))[1:]
    old_shape = struct(touched, half, rows, dtype=f32)
    index_shape = struct(touched, 8, rows, dtype=jnp.int32)
    linear_old, square_old, weight_old, where, mine, cross = kernel_call(
        functools.partial(state_kernel, owners),
        (old_shape, old_shape, old_shape, index_shape, index_shape)
        + (struct(3 * kept, half, rows, dtype=f32),),
        [VMEM] * (5 + len(packs)),
    )(step_blocks, serve_layout, linear_state, square_state, hot_slab, *late)
    cross, share_turned = lax.optimization_barrier((cross, share_turned))
    total = join([share, share_turned, rest_own], True)
    sums = early = reduce_rest(total, sizes, groups)
    cross = swap(cross, ("mp",), sizes, (1,))
    late = lax.optimization_barrier((total, *notes))[1:]
    *counts, wanted = kernel_call(
        functools.partial(side_kernel, slots, picks, active, groups, rows),
        (counts_shape,) * groups + (struct(positions * rows, requests * slots),),
        [VMEM] * (groups + 1),
    )(*late, req)
    shared = struct(kept, half, rows)
    state_shape = struct(kept, half, rows, dtype=f32)
    payload = struct(active, half, rows)
    grad_own, grad_other, new_own, linear_mid, square_mid = kernel_call(
        functools.partial(second_step_kernel, slots, picks, groups, steps, len(sums)),
        (payload, payload, shared, state_shape, state_shape),
        [VMEM] * (11 + 2 * groups + len(sums)),
    )(
        step_blocks,
        *counts,
        *notes,
        *sums,
        linear_old,
        square_old,
        weight_old,
        cross,
        hot_slab,
        slab_other,
        w1_own,
        w1_other,
        second_weight,
        head,
    )
    total = join([grad_own, swap(grad_other, ("mp",), sizes, (1,))])
    sums = reduce_rest(total, sizes, groups)
    results = (
        struct(*linear_state.shape, dtype=f32),
        struct(*square_state.shape, dtype=f32),
        struct(*serve_own.shape),
    )
    *results_at, partial = kernel_call(
        functools.partial(finish_kernel, owners, len(sums), len(early)),
        results + (struct(requests, units, dtype=f32),),
        [VMEM] * (13 + len(sums) + len(early) + len(packs)),
        [pltpu.VMEM((positions, half, rows), bf16)],
    )(
        linear_old,
        square_old,
        weight_old,
        where,
        mine,
        new_own,
        linear_mid,
        square_mid,
        wanted,
        w1_own,
        linear_state,
        square_state,
        serve_own,
        *sums,
        *early,
        *packs,
    )
    partial_other = swap(partial, ("mp",), sizes, (1,))
    linear_out, square_out, serve_out = kernel_call(
        write_kernel, results, [VMEM] * 3, [pltpu.SemaphoreType.DMA((3,))], (HBM, HBM, HBM)
    )(*results_at)
    scores = kernel_call(score_kernel, struct(1, requests, dtype=f32), [VMEM] * 4)(
        partial, partial_other, second_weight, head
    )
    return linear_out, square_out, serve_out[None], scores


def solution(mesh):
    sizes = dict(mesh.shape)
    placed = (
        P(None, "mp", None),
        P("dp", "mp", None),
        P("dp", "mp", None),
        P("replica", "dp", "mp", None),
        P(None, "mp", None),
        P(),
        P(),
        P("groups", None),
        P(None, ("groups", "dp", "replica"), None, None),
        P(None, ("groups", "dp", "replica")),
        P("replica", None),
        P("replica", ("groups", "dp"), None, None),
    )
    return jax.shard_map(
        functools.partial(local, sizes),
        mesh=mesh,
        in_specs=placed,
        out_specs=(
            P(("groups", "dp"), "mp", None),
            P(("groups", "dp"), "mp", None),
            P(("groups", "replica"), "dp", "mp", None),
            P("replica", ("groups", "dp")),
        ),
        check_vma=False,
    )
```

```python
import functools

import jax
import jax.numpy as jnp
from jax import lax
from jax.experimental import pallas as pl
from jax.experimental.pallas import tpu as pltpu
from jax.sharding import PartitionSpec as P

step_alpha = 0.5
step_beta = 1.0
sparse_penalty = 0.1
ridge_penalty = 0.05
f32 = jnp.float32
bf16 = jnp.bfloat16
VMEM = pl.BlockSpec(memory_space=pltpu.VMEM)
HBM = pl.BlockSpec(memory_space=pltpu.HBM)
nt_dims = (((1,), (1,)), ((), ()))


def kernel_call(body, out_shape, in_specs, scratch=(), out_specs=None, micros=1.0, limit=32):
    return pl.pallas_call(
        body,
        out_shape=out_shape,
        in_specs=in_specs,
        out_specs=jax.tree.map(lambda _: VMEM, out_shape) if out_specs is None else out_specs,
        scratch_shapes=list(scratch),
        compiler_params=pltpu.CompilerParams(vmem_limit_bytes=limit * 1024 * 1024),
        cost_estimate=pl.CostEstimate(
            flops=int(micros * 1e9), bytes_accessed=int(micros * 1e6), transcendentals=0
        ),
    )


def sigmoid(v):
    return 0.5 * jnp.tanh(0.5 * v) + 0.5


def ftrl_update(linear, square, gradient, current):
    grown = square + gradient * gradient
    root = jnp.sqrt(grown)
    sigma_term = (root - jnp.sqrt(square)) / step_alpha
    linear_next = linear + gradient - sigma_term * current
    shrunk = linear_next - jnp.clip(linear_next, -sparse_penalty, sparse_penalty)
    weights = -shrunk / ((step_beta + root) / step_alpha + ridge_penalty)
    return linear_next, grown, weights


def fill_counts(counts_ref, ids, column, blocks, rows):
    picks, lanes = ids.shape
    tiles = rows // 16
    level = lax.broadcasted_iota(jnp.int32, (tiles, 16, lanes), 1) + 16 * lax.broadcasted_iota(
        jnp.int32, (tiles, 16, lanes), 0
    )
    level = level.astype(f32).astype(bf16)
    wide = [jnp.broadcast_to(ids[pick : pick + 1], (16, lanes)) for pick in range(picks)]
    times = []
    for pick in range(picks):
        total = jnp.ones((16, lanes), f32)
        for later in range(pick + 1, picks):
            total = total + jnp.where(wide[later] == wide[pick], 1.0, 0.0)
        times.append(total.astype(bf16)[None])
    zero = jnp.zeros((), bf16)
    for block in range(blocks):
        filled = None
        for pick in reversed(range(picks)):
            place = (wide[pick] - float(block * rows)).astype(bf16)[None]
            filled = jnp.where(level == place, times[pick], zero if filled is None else filled)
        counts_ref[block * rows : (block + 1) * rows, column : column + lanes] = filled.reshape(
            rows, lanes
        )


def tree_sum(parts):
    parts = list(parts)
    while len(parts) > 1:
        parts = [
            parts[i] + parts[i + 1] if i + 1 < len(parts) else parts[i]
            for i in range(0, len(parts), 2)
        ]
    return parts[0]


def copies(pairs, sems):
    started = []
    for at, (source, target) in enumerate(pairs):
        copy = pltpu.make_async_copy(source, target, sems.at[at])
        copy.start()
        started.append(copy)
    return started


def lead_kernel(out_ref):
    out_ref[...] = jnp.zeros_like(out_ref)


def pick_blocks(slab_ref, blocks_ref, step, first):
    half, rows = slab_ref.shape[1:]
    tables = []
    for i in range(first, blocks_ref.shape[1]):
        chosen = jnp.broadcast_to(blocks_ref[step : step + 1, i : i + 1].astype(f32), (half, rows))
        chosen = chosen.astype(bf16)
        table = slab_ref[0]
        for block in range(1, slab_ref.shape[0]):
            table = jnp.where(chosen == jnp.asarray(block, bf16), slab_ref[block], table)
        tables.append(table)
    return jnp.concatenate(tables, axis=1)


def lead_kernel(out_ref):
    out_ref[...] = jnp.zeros_like(out_ref)


def open_kernel(lead_ref, ids_ref, labels_ref, linear_ref, square_ref, serve_ref, out_ref, pack_ref, coded_ref):
    owned = linear_ref.shape[0]
    pack_ref[0:owned] = linear_ref[...].astype(bf16)
    pack_ref[owned : 2 * owned] = square_ref[...].astype(bf16)
    pack_ref[2 * owned : 3 * owned] = serve_ref[...]
    steps, slots, picks, _ = ids_ref.shape
    samples = out_ref.shape[1]
    core = lax.axis_index("mp")
    lanes = pl.ds(pl.multiple_of(core * samples, samples), samples)
    for step in range(steps):
        for slot in range(slots):
            low = (step * slots + slot) * picks
            out_ref[low : low + picks] = ids_ref[step, slot, :, lanes].astype(f32)
    low = steps * slots * picks
    labels = labels_ref[:, lanes]
    per = slots * picks
    coded_ref[0:per] = out_ref[0:per].astype(jnp.int32) + 65536 * out_ref[per:low].astype(jnp.int32)
    fixed = jnp.floor(labels * float(1 << 30) + 0.5).astype(jnp.int32)
    coded_ref[per:] = jnp.zeros((8, samples), jnp.int32)
    coded_ref[per : per + steps] = fixed
    out_ref[low:] = jnp.zeros((8, samples), f32)
    out_ref[low : low + steps] = fixed.astype(f32) * (1.0 / (1 << 30))


def decode_note(coded_ref, note_ref, steps):
    per = coded_ref.shape[0] - 8
    pairs = coded_ref[0:per]
    note_ref[0:per] = (pairs & 65535).astype(f32)
    note_ref[per : 2 * per] = (pairs >> 16).astype(f32)
    note_ref[2 * per :] = coded_ref[per:].astype(f32) * (1.0 / (1 << 30))


def fill_step(counts_ref, note_ref, step, slots, picks, active, rows):
    samples = note_ref.shape[1]
    for slot in range(slots):
        low = (step * slots + slot) * picks
        fill_counts(counts_ref, note_ref[low : low + picks], slot * samples, active, rows)


def by_sample(pooled, slots):
    half = pooled.shape[0] // 2
    samples = pooled.shape[1] // slots
    out = []
    for low in (0, half):
        stacked = jnp.concatenate(
            [
                pooled[low : low + half, slot * samples : (slot + 1) * samples]
                for slot in range(slots)
            ],
            axis=0,
        )
        out.append(stacked.T.astype(bf16))
    return out


def network(inputs, label_rows, counts, w1_own, w1_other, w2_ref, head_ref, slots):
    half = w1_own.shape[0] // slots
    first_own, first_other, second = w1_own[...], w1_other[...], w2_ref[...]
    inputs_own = jnp.concatenate([part[0] for part in inputs], axis=0)
    inputs_other = jnp.concatenate([part[1] for part in inputs], axis=0)
    pre_one = jnp.dot(inputs_own, first_own, preferred_element_type=f32) + jnp.dot(
        inputs_other, first_other, preferred_element_type=f32
    )
    sig_one = sigmoid(pre_one)
    hidden_one = (pre_one * sig_one).astype(bf16)
    pre_two = jnp.dot(hidden_one, second, preferred_element_type=f32)
    sig_two = sigmoid(pre_two)
    hidden_two = (pre_two * sig_two).astype(bf16)
    head = head_ref[...].astype(f32)
    heads = jnp.broadcast_to(head, (128, head.shape[1])).astype(bf16)
    logit = lax.dot_general(hidden_two, heads, nt_dims, preferred_element_type=f32)
    label = jnp.concatenate(
        [jnp.broadcast_to(row, (128, row.shape[1])).T for row in label_rows], axis=0
    )
    error = sigmoid(logit) - label
    error = jnp.concatenate([error] * (head.shape[1] // 128), axis=1)
    grad_two = (error * head * (sig_two * (1.0 + pre_two * (1.0 - sig_two)))).astype(bf16)
    back = lax.dot_general(grad_two, second, nt_dims, preferred_element_type=f32)
    grad_one = (back * (sig_one * (1.0 + pre_one * (1.0 - sig_one)))).astype(bf16)
    spread = [
        lax.dot_general(first, grad_one, nt_dims, preferred_element_type=f32).astype(bf16)
        for first in (first_own, first_other)
    ]
    samples = spread[0].shape[1] // len(counts)
    total = None
    for group, group_counts in enumerate(counts):
        lanes = slice(group * samples, (group + 1) * samples)
        grad_input = jnp.concatenate(
            [
                jnp.concatenate(
                    [part[slot * half : (slot + 1) * half, lanes] for slot in range(slots)], axis=1
                )
                for part in spread
            ],
            axis=0,
        )
        grad = lax.dot_general(grad_input, group_counts, nt_dims, preferred_element_type=f32)
        grad = grad.astype(bf16).astype(f32)
        total = grad if total is None else total + grad
    return total


def first_step_kernel(slots, picks, groups, blocks_ref, note_ref, *refs):
    coded = refs[: groups - 1]
    slab_own, slab_other, w1_own, w1_other, w2_ref, head_ref = refs[groups - 1 : groups + 5]
    share_ref, rest_own, note_at, *counts_at = refs[groups + 5 :]
    active = blocks_ref.shape[1]
    half, rows = slab_other.shape[1:]
    fresh = active // 2
    kept = active - fresh
    labels = note_ref.shape[0] - 8
    table = jnp.concatenate(
        [pick_blocks(slab, blocks_ref, 0, 0) for slab in (slab_own, slab_other)], axis=0
    )
    if coded:
        decode_note(coded[0], note_at, blocks_ref.shape[0])
    inputs = []
    for note, counts_ref in zip((note_ref, note_at), counts_at):
        fill_step(counts_ref, note, 0, slots, picks, active, rows)
        pooled = jnp.dot(table, counts_ref[...], preferred_element_type=f32)
        inputs.append(by_sample(pooled, slots))
    grad = network(
        inputs,
        [note[labels : labels + 1] for note in (note_ref, note_at)[:groups]],
        [ref[...] for ref in counts_at],
        w1_own,
        w1_other,
        w2_ref,
        head_ref,
        slots,
    )
    for i in range(active):
        part = grad[:, i * rows : (i + 1) * rows].astype(bf16)
        if i < fresh:
            rest_own[i] = part[:half]
            share_ref[2 * kept + i] = part[half:]
        else:
            share_ref[i - fresh] = part[:half]
            share_ref[kept + i - fresh] = part[half:]


def side_kernel(slots, picks, groups, blocks_ref, slab_own, slab_other, *refs):
    notes = refs[:groups]
    counts_refs = refs[groups : 2 * groups]
    fresh_refs = refs[2 * groups :]
    steps, active = blocks_ref.shape
    rows = slab_own.shape[2]
    kept = active - active // 2
    table = jnp.concatenate(
        [pick_blocks(slab, blocks_ref, steps - 1, kept) for slab in (slab_own, slab_other)], axis=0
    )
    for note, counts_ref, fresh_ref in zip(notes, counts_refs, fresh_refs):
        fill_step(counts_ref, note, 1, slots, picks, active, rows)
        fresh_ref[...] = jnp.dot(table, counts_ref[kept * rows :], preferred_element_type=f32)


def wanted_kernel(rows, req_ref, wanted_ref):
    requests = req_ref.shape[0]
    lanes_ids = jnp.concatenate([req_ref[i] for i in range(requests)], axis=1).astype(f32)
    fill_counts(wanted_ref, lanes_ids, 0, wanted_ref.shape[0] // rows, rows)


def join_kernel(turned, *refs):
    *sums, out_ref = refs
    if turned:
        first, second, rest = sums
        half = (first.shape[0] - rest.shape[0]) // 2
        low = first[0:half].astype(f32) + second[half : 2 * half].astype(f32)
        high = first[half : 2 * half].astype(f32) + second[0:half].astype(f32)
        out_ref[0:half] = low.astype(bf16)
        out_ref[half : 2 * half] = high.astype(bf16)
        rest = rest[...].astype(f32) + second[2 * half :].astype(f32)
        out_ref[2 * half :] = rest.astype(bf16)
    else:
        out_ref[...] = tree_sum([part[...].astype(f32) for part in sums]).astype(bf16)


def tree_sum(parts):
    parts = list(parts)
    while len(parts) > 1:
        parts = [
            parts[i] + parts[i + 1] if i + 1 < len(parts) else parts[i]
            for i in range(0, len(parts), 2)
        ]
    return parts[0]


def old_state(block, me, owners, linear_ref, square_ref, slab_own, packs):
    owned, half, rows = linear_ref.shape
    linear = jnp.zeros((half, rows), f32)
    square = jnp.zeros((half, rows), f32)
    weight = jnp.zeros((half, rows), f32)
    gathered = len(packs) == 1
    for k in range(owners):
        for place in range(owned):
            here = k * owned + place
            weight = jnp.where(block == here, slab_own[here].astype(f32), weight)
            if gathered:
                hit = block == here
                old = packs[0][k, place].astype(f32), packs[0][k, owned + place].astype(f32)
            else:
                hit = block == (me ^ k) * owned + place
                if k == 0:
                    old = linear_ref[place], square_ref[place]
                else:
                    pack = packs[k - 1]
                    old = (
                        pack[place].astype(f32),
                        pack[owned + place].astype(f32),
                    )
            linear = jnp.where(hit, old[0], linear)
            square = jnp.where(hit, old[1], square)
    if gathered:
        for place in range(owned):
            hit = block == me * owned + place
            linear = jnp.where(hit, linear_ref[place], linear)
            square = jnp.where(hit, square_ref[place], square)
    return linear, square, weight


def state_kernel(owners, blocks_ref, layout_ref, linear_ref, square_ref, slab_own, *refs):
    packs = refs[:-6]
    linear_out, square_out, weight_out, where_out, mine_out, cross_out = refs[-6:]
    active = blocks_ref.shape[1]
    owned, half, rows = linear_ref.shape
    fresh = active // 2
    kept = active - fresh
    me = lax.axis_index("dp")
    for i in range(active + fresh):
        step, at = (1, i) if i < active else (0, i - active)
        block = jnp.broadcast_to(blocks_ref[step : step + 1, at : at + 1], (8, rows))
        wide = jnp.broadcast_to(block[0:1], (half, rows))
        old = old_state(wide, me, owners, linear_ref, square_ref, slab_own, packs)
        linear_out[i], square_out[i], weight_out[i] = old
        if i < kept:
            cross_out[i], cross_out[kept + i], cross_out[2 * kept + i] = old
        owner = block // owned
        place = block % owned
        turn = (owner + place) % owners
        home = jnp.zeros_like(block)
        for q in range(owners):
            home = jnp.where(turn == q, layout_ref[0:1, q : q + 1], home)
        where_out[i] = home * owned + place
        mine_out[i] = jnp.where(owner == me, place, -1)


def second_step_kernel(slots, picks, groups, steps, sums_count, blocks_ref, *refs):
    counts_refs = refs[:groups]
    fresh_refs = refs[groups : 2 * groups]
    notes = refs[2 * groups : 3 * groups]
    sums = refs[3 * groups : 3 * groups + sums_count]
    refs = refs[3 * groups + sums_count :]
    linear_own, square_own, weight_own, cross = refs[:4]
    w1_own, w1_other, w2_ref, head_ref = refs[4:8]
    out_own, out_other, new_out, linear_out, square_out = refs[8:]
    active = blocks_ref.shape[1]
    half, rows = cross.shape[1:]
    fresh = active // 2
    kept = active - fresh
    labels = notes[0].shape[0] - 8 + steps - 1

    new_own, new_other = [], []
    for i in range(kept):
        gradient = tree_sum([part[i].astype(f32) for part in sums])
        linear, square, weights = ftrl_update(linear_own[i], square_own[i], gradient, weight_own[i])
        linear_out[i] = linear
        square_out[i] = square
        new_own.append(weights.astype(bf16))
        new_out[i] = new_own[i]
        gradient = tree_sum([part[kept + i].astype(f32) for part in sums])
        weights = ftrl_update(cross[i], cross[kept + i], gradient, cross[2 * kept + i])[2]
        new_other.append(weights.astype(bf16))

    new = [jnp.concatenate(blocks, axis=1) for blocks in (new_own, new_other)]
    table = jnp.concatenate(new, axis=0)
    counts = [ref[...] for ref in counts_refs]
    inputs = [
        by_sample(
            fresh_ref[...] + jnp.dot(table, group[: kept * rows], preferred_element_type=f32), slots
        )
        for group, fresh_ref in zip(counts, fresh_refs)
    ]
    grad = network(
        inputs,
        [note[labels : labels + 1] for note in notes],
        counts,
        w1_own,
        w1_other,
        w2_ref,
        head_ref,
        slots,
    )
    for i in range(active):
        part = grad[:, i * rows : (i + 1) * rows].astype(bf16)
        out_own[i] = part[:half]
        out_other[i] = part[half:]


def finish_kernel(owners, sums_count, early_count, *refs):
    linear_old, square_old, weight_old, where_ref, mine_ref = refs[:5]
    new_ref, linear_mid, square_mid, counts_ref, w1_own = refs[5:10]
    linear_in, square_in, serve_in = refs[10:13]
    sums = refs[13 : 13 + sums_count]
    early = refs[13 + sums_count : 13 + sums_count + early_count]
    packs = refs[13 + sums_count + early_count : -5]
    linear_at, square_at, serve_at, partial_out, table_at = refs[-5:]
    touched, _, rows = where_ref.shape
    owned, half, _ = linear_in.shape
    kept = new_ref.shape[0]
    active = sums[0].shape[0]
    positions = table_at.shape[0]
    me = lax.axis_index("dp")
    for k in range(owners):
        if len(packs) == 1:
            table_at[k * owned : (k + 1) * owned] = packs[0][k, 2 * owned : 3 * owned]
        elif k == 0:
            table_at[pl.ds(me * owned, owned)] = serve_in[...]
        else:
            table_at[pl.ds((me ^ k) * owned, owned)] = packs[k - 1][2 * owned : 3 * owned]
    weights, linears, squares = [], [], []
    for i in range(touched):
        parts = [p[i] for p in sums] if i < active else [p[2 * kept + i - active] for p in early]
        gradient = tree_sum([part.astype(f32) for part in parts])
        if i < kept:
            old = linear_mid[i], square_mid[i], new_ref[i].astype(f32)
        else:
            old = linear_old[i], square_old[i], weight_old[i]
        linear, square, weight = ftrl_update(old[0], old[1], gradient, old[2])
        linears.append(linear)
        squares.append(square)
        weights.append(weight)

    def wide(ref, i):
        return jnp.broadcast_to(ref[i][0:1], (half, rows))

    home = [wide(mine_ref, i) for i in range(touched)]
    goal = [wide(where_ref, i) for i in range(touched)]
    for place in range(owned):
        linear, square = linear_in[place], square_in[place]
        serve = serve_in[place].astype(f32)
        for i in range(touched):
            hit = home[i] == place
            linear = jnp.where(hit, linears[i], linear)
            square = jnp.where(hit, squares[i], square)
            serve = jnp.where(goal[i] == me * owned + place, weights[i], serve)
        linear_at[place] = linear
        square_at[place] = square
        serve_at[place] = serve.astype(bf16)
    tables = []
    for position in range(positions):
        table = table_at[position].astype(f32)
        for i in range(touched):
            table = jnp.where(goal[i] == position, weights[i], table)
        tables.append(table.astype(bf16))
    pooled = jnp.dot(jnp.concatenate(tables, axis=1), counts_ref[...], preferred_element_type=f32)
    units = w1_own.shape[1]
    slots = w1_own.shape[0] // half
    requests = counts_ref.shape[1] // slots
    stacked = jnp.concatenate([pooled] * slots, axis=0)
    wanted = lax.broadcasted_iota(jnp.int32, stacked.shape, 0) // half
    present = lax.broadcasted_iota(jnp.int32, stacked.shape, 1) % slots
    stacked = jnp.where(wanted == present, stacked, 0.0)
    product = jnp.dot(stacked.T.astype(bf16), w1_own[...], preferred_element_type=f32)
    partial_out[...] = jnp.sum(product.reshape(requests, slots, units), axis=1)


def write_kernel(*refs):
    count = len(refs) // 2
    for copy in copies(list(zip(refs[:count], refs[count : 2 * count])), refs[-1]):
        copy.wait()


def score_kernel(own_ref, other_ref, w2_ref, head_ref, out_ref):
    pre_one = own_ref[...] + other_ref[...]
    hidden_one = (pre_one * sigmoid(pre_one)).astype(bf16)
    pre_two = jnp.dot(hidden_one, w2_ref[...], preferred_element_type=f32)
    hidden_two = (pre_two * sigmoid(pre_two)).astype(bf16)
    heads = jnp.broadcast_to(head_ref[...].astype(f32), (8, head_ref.shape[1])).astype(bf16)
    logit = lax.dot_general(heads, hidden_two, nt_dims, preferred_element_type=f32)
    out_ref[...] = logit[0:1]


def swap(value, axes, sizes, bits):
    shape = tuple(sizes[a] for a in axes)
    count = 1
    for size in shape:
        count *= size
    pairs = []
    for index in range(count):
        rest, coords = index, []
        for size in reversed(shape):
            coords.append(rest % size)
            rest //= size
        coords = coords[::-1]
        target = 0
        for coord, bit, size in zip(coords, bits, shape):
            target = target * size + (coord ^ bit)
        pairs.append((index, target))
    return lax.ppermute(value, axes, pairs)


def join(parts, turned=False):
    return kernel_call(
        functools.partial(join_kernel, turned),
        jax.ShapeDtypeStruct(parts[0].shape, bf16),
        [VMEM] * len(parts),
    )(*parts)


def reduce_rest(total, sizes, groups):
    parts = [total]
    bit = groups
    while bit < sizes["replica"]:
        total = join(parts) if len(parts) > 1 else total
        parts = [total, swap(total, ("replica",), sizes, (bit,))]
        bit *= 2
    bit = 1
    while bit < sizes["dp"]:
        total = join(parts) if len(parts) > 1 else total
        steps = [k * bit for k in range(1, 4) if k * bit < sizes["dp"]]
        parts = [total] + [swap(total, ("dp",), sizes, (k,)) for k in steps]
        bit *= 4
    return parts


def local(
    sizes,
    hot_slab,
    linear_state,
    square_state,
    serve_table,
    first_weight,
    second_weight,
    out_weight,
    step_blocks,
    feature_ids,
    click_labels,
    serve_layout,
    request_ids,
):
    owners = sizes["dp"]
    owned, half, rows = linear_state.shape
    steps, active = step_blocks.shape
    fresh = active // 2
    kept = active - fresh
    touched = active + fresh
    samples = feature_ids.shape[1] // sizes["mp"]
    slots, picks = feature_ids.shape[2:]
    units = first_weight.shape[2]
    ids = jnp.transpose(feature_ids, (0, 2, 3, 1))
    req = jnp.transpose(request_ids[0], (0, 2, 1))
    requests = req.shape[0]
    positions = owners * owned
    groups = 2 if sizes["replica"] > 1 else 1
    direct = owners == 4

    def struct(*shape, dtype=bf16):
        return jax.ShapeDtypeStruct(shape, dtype)

    w1_own = first_weight.reshape(-1, units)
    w1_other = swap(w1_own, ("mp",), sizes, (1,))
    slab_other = swap(hot_slab, ("mp",), sizes, (1,))
    head = out_weight.reshape(1, -1)
    serve_own = serve_table[0]

    lead = kernel_call(lead_kernel, struct(8, 128, dtype=f32), [], micros=20.0)()
    per = slots * picks
    note, pack, coded = kernel_call(
        open_kernel,
        (
            struct(steps * per + 8, samples, dtype=f32),
            struct(3 * owned, half, rows),
            struct(per + 8, samples, dtype=jnp.int32),
        ),
        [VMEM] * 6,
    )(lead, ids, click_labels, linear_state, square_state, serve_own)
    if direct:
        packs = [swap(pack, ("dp",), sizes, (k,)) for k in range(1, owners)]
    else:
        packs = [lax.all_gather(pack, "dp", axis=0, tiled=False)]
    coded = [swap(coded, ("replica",), sizes, (1,))] if groups > 1 else []
    counts_shape = struct(active * rows, slots * samples)
    others = struct(fresh, half, rows)
    share, rest_own, note_other = kernel_call(
        functools.partial(first_step_kernel, slots, picks, groups),
        (struct(2 * kept + fresh, half, rows), others, struct(*note.shape, dtype=f32)),
        [VMEM] * (7 + groups),
        [pltpu.VMEM(counts_shape.shape, bf16)] * groups,
    )(
        step_blocks,
        note,
        *coded,
        hot_slab,
        slab_other,
        w1_own,
        w1_other,
        second_weight,
        head,
    )
    notes = [note, note_other][:groups]
    share_turned = swap(share, ("mp",), sizes, (1,))
    late = lax.optimization_barrier((share, *packs))[1:]
    old_shape = struct(touched, half, rows, dtype=f32)
    index_shape = struct(touched, 8, rows, dtype=jnp.int32)
    linear_old, square_old, weight_old, where, mine, cross = kernel_call(
        functools.partial(state_kernel, owners),
        (old_shape, old_shape, old_shape, index_shape, index_shape)
        + (struct(3 * kept, half, rows, dtype=f32),),
        [VMEM] * (5 + len(packs)),
    )(step_blocks, serve_layout, linear_state, square_state, hot_slab, *late)
    cross, share_turned = lax.optimization_barrier((cross, share_turned))
    total = join([share, share_turned, rest_own], True)
    sums = early = reduce_rest(total, sizes, groups)
    cross = swap(cross, ("mp",), sizes, (1,))
    late = lax.optimization_barrier((total, *notes))[1:]
    counts = kernel_call(
        functools.partial(side_kernel, slots, picks, groups),
        (counts_shape,) * groups
        + (struct(2 * half, slots * samples, dtype=f32),) * groups,
        [VMEM] * (groups + 3),
    )(step_blocks, hot_slab, slab_other, *late)
    shared = struct(kept, half, rows)
    state_shape = struct(kept, half, rows, dtype=f32)
    payload = struct(active, half, rows)
    grad_own, grad_other, new_own, linear_mid, square_mid = kernel_call(
        functools.partial(second_step_kernel, slots, picks, groups, steps, len(sums)),
        (payload, payload, shared, state_shape, state_shape),
        [VMEM] * (9 + 3 * groups + len(sums)),
    )(
        step_blocks,
        *counts,
        *notes,
        *sums,
        linear_old,
        square_old,
        weight_old,
        cross,
        w1_own,
        w1_other,
        second_weight,
        head,
    )
    total = join([grad_own, swap(grad_other, ("mp",), sizes, (1,))])
    sums = reduce_rest(total, sizes, groups)
    late = lax.optimization_barrier((total, req))[1]
    wanted = kernel_call(
        functools.partial(wanted_kernel, rows), struct(positions * rows, requests * slots), [VMEM]
    )(late)
    results = (
        struct(*linear_state.shape, dtype=f32),
        struct(*square_state.shape, dtype=f32),
        struct(*serve_own.shape),
    )
    *results_at, partial = kernel_call(
        functools.partial(finish_kernel, owners, len(sums), len(early)),
        results + (struct(requests, units, dtype=f32),),
        [VMEM] * (13 + len(sums) + len(early) + len(packs)),
        [pltpu.VMEM((positions, half, rows), bf16)],
    )(
        linear_old,
        square_old,
        weight_old,
        where,
        mine,
        new_own,
        linear_mid,
        square_mid,
        wanted,
        w1_own,
        linear_state,
        square_state,
        serve_own,
        *sums,
        *early,
        *packs,
    )
    partial_other = swap(partial, ("mp",), sizes, (1,))
    linear_out, square_out, serve_out = kernel_call(
        write_kernel, results, [VMEM] * 3, [pltpu.SemaphoreType.DMA((3,))], (HBM, HBM, HBM)
    )(*results_at)
    scores = kernel_call(score_kernel, struct(1, requests, dtype=f32), [VMEM] * 4)(
        partial, partial_other, second_weight, head
    )
    return linear_out, square_out, serve_out[None], scores


def solution(mesh):
    sizes = dict(mesh.shape)
    placed = (
        P(None, "mp", None),
        P("dp", "mp", None),
        P("dp", "mp", None),
        P("replica", "dp", "mp", None),
        P(None, "mp", None),
        P(),
        P(),
        P("groups", None),
        P(None, ("groups", "dp", "replica"), None, None),
        P(None, ("groups", "dp", "replica")),
        P("replica", None),
        P("replica", ("groups", "dp"), None, None),
    )
    return jax.shard_map(
        functools.partial(local, sizes),
        mesh=mesh,
        in_specs=placed,
        out_specs=(
            P(("groups", "dp"), "mp", None),
            P(("groups", "dp"), "mp", None),
            P(("groups", "replica"), "dp", "mp", None),
            P("replica", ("groups", "dp")),
        ),
        check_vma=False,
    )
```

```python
import functools

import jax
import jax.numpy as jnp
from jax import lax
from jax.experimental import pallas as pl
from jax.experimental.pallas import tpu as pltpu
from jax.sharding import PartitionSpec as P

step_alpha = 0.5
step_beta = 1.0
sparse_penalty = 0.1
ridge_penalty = 0.05
f32 = jnp.float32
bf16 = jnp.bfloat16
VMEM = pl.BlockSpec(memory_space=pltpu.VMEM)
HBM = pl.BlockSpec(memory_space=pltpu.HBM)
nt_dims = (((1,), (1,)), ((), ()))


def kernel_call(body, out_shape, in_specs, scratch=(), out_specs=None, micros=1.0, limit=32):
    return pl.pallas_call(
        body,
        out_shape=out_shape,
        in_specs=in_specs,
        out_specs=jax.tree.map(lambda _: VMEM, out_shape) if out_specs is None else out_specs,
        scratch_shapes=list(scratch),
        compiler_params=pltpu.CompilerParams(vmem_limit_bytes=limit * 1024 * 1024),
        cost_estimate=pl.CostEstimate(
            flops=int(micros * 1e9), bytes_accessed=int(micros * 1e6), transcendentals=0
        ),
    )


def sigmoid(v):
    return 0.5 * jnp.tanh(0.5 * v) + 0.5


def ftrl_update(linear, square, gradient, current):
    grown = square + gradient * gradient
    root = jnp.sqrt(grown)
    sigma_term = (root - jnp.sqrt(square)) / step_alpha
    linear_next = linear + gradient - sigma_term * current
    shrunk = linear_next - jnp.clip(linear_next, -sparse_penalty, sparse_penalty)
    weights = -shrunk / ((step_beta + root) / step_alpha + ridge_penalty)
    return linear_next, grown, weights


def fill_counts(counts_ref, ids, column, blocks, rows):
    picks, lanes = ids.shape
    tiles = rows // 16
    level = lax.broadcasted_iota(jnp.int32, (tiles, 16, lanes), 1) + 16 * lax.broadcasted_iota(
        jnp.int32, (tiles, 16, lanes), 0
    )
    level = level.astype(f32).astype(bf16)
    wide = [jnp.broadcast_to(ids[pick : pick + 1], (16, lanes)) for pick in range(picks)]
    times = []
    for pick in range(picks):
        total = jnp.ones((16, lanes), f32)
        for later in range(pick + 1, picks):
            total = total + jnp.where(wide[later] == wide[pick], 1.0, 0.0)
        times.append(total.astype(bf16)[None])
    zero = jnp.zeros((), bf16)
    for block in range(blocks):
        filled = None
        for pick in reversed(range(picks)):
            place = (wide[pick] - float(block * rows)).astype(bf16)[None]
            filled = jnp.where(level == place, times[pick], zero if filled is None else filled)
        counts_ref[block * rows : (block + 1) * rows, column : column + lanes] = filled.reshape(
            rows, lanes
        )


def tree_sum(parts):
    parts = list(parts)
    while len(parts) > 1:
        parts = [
            parts[i] + parts[i + 1] if i + 1 < len(parts) else parts[i]
            for i in range(0, len(parts), 2)
        ]
    return parts[0]


def copies(pairs, sems):
    started = []
    for at, (source, target) in enumerate(pairs):
        copy = pltpu.make_async_copy(source, target, sems.at[at])
        copy.start()
        started.append(copy)
    return started


def lead_kernel(out_ref):
    out_ref[...] = jnp.zeros_like(out_ref)


def pick_blocks(slab_ref, blocks_ref, step, first):
    half, rows = slab_ref.shape[1:]
    tables = []
    for i in range(first, blocks_ref.shape[1]):
        chosen = jnp.broadcast_to(blocks_ref[step : step + 1, i : i + 1].astype(f32), (half, rows))
        chosen = chosen.astype(bf16)
        table = slab_ref[0]
        for block in range(1, slab_ref.shape[0]):
            table = jnp.where(chosen == jnp.asarray(block, bf16), slab_ref[block], table)
        tables.append(table)
    return jnp.concatenate(tables, axis=1)


def lead_kernel(out_ref):
    out_ref[...] = jnp.zeros_like(out_ref)


def open_kernel(lead_ref, ids_ref, labels_ref, linear_ref, square_ref, serve_ref, out_ref, pack_ref, coded_ref):
    owned = linear_ref.shape[0]
    pack_ref[0:owned] = linear_ref[...].astype(bf16)
    pack_ref[owned : 2 * owned] = square_ref[...].astype(bf16)
    pack_ref[2 * owned : 3 * owned] = serve_ref[...]
    steps, slots, picks, _ = ids_ref.shape
    samples = out_ref.shape[1]
    core = lax.axis_index("mp")
    lanes = pl.ds(pl.multiple_of(core * samples, samples), samples)
    for step in range(steps):
        for slot in range(slots):
            low = (step * slots + slot) * picks
            out_ref[low : low + picks] = ids_ref[step, slot, :, lanes].astype(f32)
    low = steps * slots * picks
    labels = labels_ref[:, lanes]
    per = slots * picks
    coded_ref[0:per] = out_ref[0:per].astype(jnp.int32) + 65536 * out_ref[per:low].astype(jnp.int32)
    fixed = jnp.floor(labels * float(1 << 30) + 0.5).astype(jnp.int32)
    coded_ref[per:] = jnp.zeros((8, samples), jnp.int32)
    coded_ref[per : per + steps] = fixed
    out_ref[low:] = jnp.zeros((8, samples), f32)
    out_ref[low : low + steps] = fixed.astype(f32) * (1.0 / (1 << 30))


def decode_note(coded_ref, note_ref, steps):
    per = coded_ref.shape[0] - 8
    pairs = coded_ref[0:per]
    note_ref[0:per] = (pairs & 65535).astype(f32)
    note_ref[per : 2 * per] = (pairs >> 16).astype(f32)
    note_ref[2 * per :] = coded_ref[per:].astype(f32) * (1.0 / (1 << 30))


def fill_step(counts_ref, note_ref, step, slots, picks, active, rows):
    samples = note_ref.shape[1]
    for slot in range(slots):
        low = (step * slots + slot) * picks
        fill_counts(counts_ref, note_ref[low : low + picks], slot * samples, active, rows)


def by_sample(pooled, slots):
    half = pooled.shape[0] // 2
    samples = pooled.shape[1] // slots
    out = []
    for low in (0, half):
        stacked = jnp.concatenate(
            [
                pooled[low : low + half, slot * samples : (slot + 1) * samples]
                for slot in range(slots)
            ],
            axis=0,
        )
        out.append(stacked.T.astype(bf16))
    return out


def network(inputs, label_rows, counts, w1_own, w1_other, w2_ref, head_ref, slots):
    half = w1_own.shape[0] // slots
    first_own, first_other, second = w1_own[...], w1_other[...], w2_ref[...]
    inputs_own = jnp.concatenate([part[0] for part in inputs], axis=0)
    inputs_other = jnp.concatenate([part[1] for part in inputs], axis=0)
    pre_one = jnp.dot(inputs_own, first_own, preferred_element_type=f32) + jnp.dot(
        inputs_other, first_other, preferred_element_type=f32
    )
    sig_one = sigmoid(pre_one)
    hidden_one = (pre_one * sig_one).astype(bf16)
    pre_two = jnp.dot(hidden_one, second, preferred_element_type=f32)
    sig_two = sigmoid(pre_two)
    hidden_two = (pre_two * sig_two).astype(bf16)
    head = head_ref[...].astype(f32)
    heads = jnp.broadcast_to(head, (128, head.shape[1])).astype(bf16)
    logit = lax.dot_general(hidden_two, heads, nt_dims, preferred_element_type=f32)
    label = jnp.concatenate(
        [jnp.broadcast_to(row, (128, row.shape[1])).T for row in label_rows], axis=0
    )
    error = sigmoid(logit) - label
    error = jnp.concatenate([error] * (head.shape[1] // 128), axis=1)
    grad_two = (error * head * (sig_two * (1.0 + pre_two * (1.0 - sig_two)))).astype(bf16)
    back = lax.dot_general(grad_two, second, nt_dims, preferred_element_type=f32)
    grad_one = (back * (sig_one * (1.0 + pre_one * (1.0 - sig_one)))).astype(bf16)
    spread = [
        lax.dot_general(first, grad_one, nt_dims, preferred_element_type=f32).astype(bf16)
        for first in (first_own, first_other)
    ]
    samples = spread[0].shape[1] // len(counts)
    total = None
    for group, group_counts in enumerate(counts):
        lanes = slice(group * samples, (group + 1) * samples)
        grad_input = jnp.concatenate(
            [
                jnp.concatenate(
                    [part[slot * half : (slot + 1) * half, lanes] for slot in range(slots)], axis=1
                )
                for part in spread
            ],
            axis=0,
        )
        grad = lax.dot_general(grad_input, group_counts, nt_dims, preferred_element_type=f32)
        grad = grad.astype(bf16).astype(f32)
        total = grad if total is None else total + grad
    return total


def first_step_kernel(slots, picks, groups, blocks_ref, note_ref, *refs):
    coded = refs[: groups - 1]
    slab_own, slab_other, w1_own, w1_other, w2_ref, head_ref = refs[groups - 1 : groups + 5]
    share_ref, rest_own, note_at, *counts_at = refs[groups + 5 :]
    active = blocks_ref.shape[1]
    half, rows = slab_other.shape[1:]
    fresh = active // 2
    kept = active - fresh
    labels = note_ref.shape[0] - 8
    table = jnp.concatenate(
        [pick_blocks(slab, blocks_ref, 0, 0) for slab in (slab_own, slab_other)], axis=0
    )
    if coded:
        decode_note(coded[0], note_at, blocks_ref.shape[0])
    inputs = []
    for note, counts_ref in zip((note_ref, note_at), counts_at):
        fill_step(counts_ref, note, 0, slots, picks, active, rows)
        pooled = jnp.dot(table, counts_ref[...], preferred_element_type=f32)
        inputs.append(by_sample(pooled, slots))
    grad = network(
        inputs,
        [note[labels : labels + 1] for note in (note_ref, note_at)[:groups]],
        [ref[...] for ref in counts_at],
        w1_own,
        w1_other,
        w2_ref,
        head_ref,
        slots,
    )
    for i in range(active):
        part = grad[:, i * rows : (i + 1) * rows].astype(bf16)
        if i < fresh:
            rest_own[i] = part[:half]
            share_ref[2 * kept + i] = part[half:]
        else:
            share_ref[i - fresh] = part[:half]
            share_ref[kept + i - fresh] = part[half:]


def side_kernel(slots, picks, groups, blocks_ref, slab_own, slab_other, *refs):
    notes = refs[:groups]
    counts_refs = refs[groups : 2 * groups]
    fresh_refs = refs[2 * groups :]
    steps, active = blocks_ref.shape
    rows = slab_own.shape[2]
    kept = active - active // 2
    table = jnp.concatenate(
        [pick_blocks(slab, blocks_ref, steps - 1, kept) for slab in (slab_own, slab_other)], axis=0
    )
    for note, counts_ref, fresh_ref in zip(notes, counts_refs, fresh_refs):
        fill_step(counts_ref, note, 1, slots, picks, active, rows)
        fresh_ref[...] = jnp.dot(table, counts_ref[kept * rows :], preferred_element_type=f32)


def wanted_kernel(rows, req_ref, wanted_ref):
    requests = req_ref.shape[0]
    lanes_ids = jnp.concatenate([req_ref[i] for i in range(requests)], axis=1).astype(f32)
    fill_counts(wanted_ref, lanes_ids, 0, wanted_ref.shape[0] // rows, rows)


def join_kernel(turned, *refs):
    *sums, out_ref = refs
    if turned:
        first, second, rest = sums
        half = (first.shape[0] - rest.shape[0]) // 2
        low = first[0:half].astype(f32) + second[half : 2 * half].astype(f32)
        high = first[half : 2 * half].astype(f32) + second[0:half].astype(f32)
        out_ref[0:half] = low.astype(bf16)
        out_ref[half : 2 * half] = high.astype(bf16)
        rest = rest[...].astype(f32) + second[2 * half :].astype(f32)
        out_ref[2 * half :] = rest.astype(bf16)
    else:
        out_ref[...] = tree_sum([part[...].astype(f32) for part in sums]).astype(bf16)


def tree_sum(parts):
    parts = list(parts)
    while len(parts) > 1:
        parts = [
            parts[i] + parts[i + 1] if i + 1 < len(parts) else parts[i]
            for i in range(0, len(parts), 2)
        ]
    return parts[0]


def old_state(block, me, owners, linear_ref, square_ref, slab_own, packs):
    owned, half, rows = linear_ref.shape
    linear = jnp.zeros((half, rows), f32)
    square = jnp.zeros((half, rows), f32)
    weight = jnp.zeros((half, rows), f32)
    gathered = len(packs) == 1
    for k in range(owners):
        for place in range(owned):
            here = k * owned + place
            weight = jnp.where(block == here, slab_own[here].astype(f32), weight)
            if gathered:
                hit = block == here
                old = packs[0][k, place].astype(f32), packs[0][k, owned + place].astype(f32)
            else:
                hit = block == (me ^ k) * owned + place
                if k == 0:
                    old = linear_ref[place], square_ref[place]
                else:
                    pack = packs[k - 1]
                    old = (
                        pack[place].astype(f32),
                        pack[owned + place].astype(f32),
                    )
            linear = jnp.where(hit, old[0], linear)
            square = jnp.where(hit, old[1], square)
    if gathered:
        for place in range(owned):
            hit = block == me * owned + place
            linear = jnp.where(hit, linear_ref[place], linear)
            square = jnp.where(hit, square_ref[place], square)
    return linear, square, weight


def shared_kernel(owners, blocks_ref, linear_ref, square_ref, slab_own, *refs):
    packs = refs[:-4]
    linear_out, square_out, weight_out, cross_out = refs[-4:]
    active = blocks_ref.shape[1]
    half, rows = linear_ref.shape[1:]
    kept = linear_out.shape[0]
    me = lax.axis_index("dp")
    for i in range(kept):
        at = active - kept + i
        block = jnp.broadcast_to(blocks_ref[0:1, at : at + 1], (half, rows))
        old = old_state(block, me, owners, linear_ref, square_ref, slab_own, packs)
        linear_out[i], square_out[i], weight_out[i] = old
        cross_out[i], cross_out[kept + i], cross_out[2 * kept + i] = old


def state_kernel(owners, blocks_ref, layout_ref, linear_ref, square_ref, slab_own, *refs):
    packs = refs[:-5]
    linear_out, square_out, weight_out, where_out, mine_out = refs[-5:]
    active = blocks_ref.shape[1]
    owned, half, rows = linear_ref.shape
    fresh = active // 2
    kept = active - fresh
    me = lax.axis_index("dp")
    for i in range(active + fresh):
        step, at = (1, i) if i < active else (0, i - active)
        block = jnp.broadcast_to(blocks_ref[step : step + 1, at : at + 1], (8, rows))
        if i >= kept:
            wide = jnp.broadcast_to(block[0:1], (half, rows))
            old = old_state(wide, me, owners, linear_ref, square_ref, slab_own, packs)
            linear_out[i - kept], square_out[i - kept], weight_out[i - kept] = old
        owner = block // owned
        place = block % owned
        turn = (owner + place) % owners
        home = jnp.zeros_like(block)
        for q in range(owners):
            home = jnp.where(turn == q, layout_ref[0:1, q : q + 1], home)
        where_out[i] = home * owned + place
        mine_out[i] = jnp.where(owner == me, place, -1)


def second_step_kernel(slots, picks, groups, steps, sums_count, blocks_ref, *refs):
    counts_refs = refs[:groups]
    fresh_refs = refs[groups : 2 * groups]
    notes = refs[2 * groups : 3 * groups]
    sums = refs[3 * groups : 3 * groups + sums_count]
    refs = refs[3 * groups + sums_count :]
    linear_own, square_own, weight_own, cross = refs[:4]
    w1_own, w1_other, w2_ref, head_ref = refs[4:8]
    out_own, out_other, new_out, linear_out, square_out = refs[8:]
    active = blocks_ref.shape[1]
    half, rows = cross.shape[1:]
    fresh = active // 2
    kept = active - fresh
    labels = notes[0].shape[0] - 8 + steps - 1

    new_own, new_other = [], []
    for i in range(kept):
        gradient = tree_sum([part[i].astype(f32) for part in sums])
        linear, square, weights = ftrl_update(linear_own[i], square_own[i], gradient, weight_own[i])
        linear_out[i] = linear
        square_out[i] = square
        new_own.append(weights.astype(bf16))
        new_out[i] = new_own[i]
        gradient = tree_sum([part[kept + i].astype(f32) for part in sums])
        weights = ftrl_update(cross[i], cross[kept + i], gradient, cross[2 * kept + i])[2]
        new_other.append(weights.astype(bf16))

    new = [jnp.concatenate(blocks, axis=1) for blocks in (new_own, new_other)]
    table = jnp.concatenate(new, axis=0)
    counts = [ref[...] for ref in counts_refs]
    inputs = [
        by_sample(
            fresh_ref[...] + jnp.dot(table, group[: kept * rows], preferred_element_type=f32), slots
        )
        for group, fresh_ref in zip(counts, fresh_refs)
    ]
    grad = network(
        inputs,
        [note[labels : labels + 1] for note in notes],
        counts,
        w1_own,
        w1_other,
        w2_ref,
        head_ref,
        slots,
    )
    for i in range(active):
        part = grad[:, i * rows : (i + 1) * rows].astype(bf16)
        out_own[i] = part[:half]
        out_other[i] = part[half:]


def finish_kernel(owners, sums_count, early_count, *refs):
    linear_old, square_old, weight_old, where_ref, mine_ref = refs[:5]
    new_ref, linear_mid, square_mid, counts_ref, w1_own = refs[5:10]
    linear_in, square_in, serve_in = refs[10:13]
    sums = refs[13 : 13 + sums_count]
    early = refs[13 + sums_count : 13 + sums_count + early_count]
    packs = refs[13 + sums_count + early_count : -5]
    linear_at, square_at, serve_at, partial_out, table_at = refs[-5:]
    touched, _, rows = where_ref.shape
    owned, half, _ = linear_in.shape
    kept = new_ref.shape[0]
    active = sums[0].shape[0]
    positions = table_at.shape[0]
    me = lax.axis_index("dp")
    for k in range(owners):
        if len(packs) == 1:
            table_at[k * owned : (k + 1) * owned] = packs[0][k, 2 * owned : 3 * owned]
        elif k == 0:
            table_at[pl.ds(me * owned, owned)] = serve_in[...]
        else:
            table_at[pl.ds((me ^ k) * owned, owned)] = packs[k - 1][2 * owned : 3 * owned]
    weights, linears, squares = [], [], []
    for i in range(touched):
        parts = [p[i] for p in sums] if i < active else [p[2 * kept + i - active] for p in early]
        gradient = tree_sum([part.astype(f32) for part in parts])
        if i < kept:
            old = linear_mid[i], square_mid[i], new_ref[i].astype(f32)
        else:
            old = linear_old[i - kept], square_old[i - kept], weight_old[i - kept]
        linear, square, weight = ftrl_update(old[0], old[1], gradient, old[2])
        linears.append(linear)
        squares.append(square)
        weights.append(weight)

    def wide(ref, i):
        return jnp.broadcast_to(ref[i][0:1], (half, rows))

    home = [wide(mine_ref, i) for i in range(touched)]
    goal = [wide(where_ref, i) for i in range(touched)]
    for place in range(owned):
        linear, square = linear_in[place], square_in[place]
        serve = serve_in[place].astype(f32)
        for i in range(touched):
            hit = home[i] == place
            linear = jnp.where(hit, linears[i], linear)
            square = jnp.where(hit, squares[i], square)
            serve = jnp.where(goal[i] == me * owned + place, weights[i], serve)
        linear_at[place] = linear
        square_at[place] = square
        serve_at[place] = serve.astype(bf16)
    tables = []
    for position in range(positions):
        table = table_at[position].astype(f32)
        for i in range(touched):
            table = jnp.where(goal[i] == position, weights[i], table)
        tables.append(table.astype(bf16))
    pooled = jnp.dot(jnp.concatenate(tables, axis=1), counts_ref[...], preferred_element_type=f32)
    units = w1_own.shape[1]
    slots = w1_own.shape[0] // half
    requests = counts_ref.shape[1] // slots
    copies_high = 128 // half
    turned = jnp.concatenate([pooled] * copies_high, axis=0).T
    spread = jnp.concatenate([turned] * (slots // copies_high), axis=1)
    wanted = lax.broadcasted_iota(jnp.int32, spread.shape, 1) // half
    present = lax.broadcasted_iota(jnp.int32, spread.shape, 0) % slots
    spread = jnp.where(wanted == present, spread, 0.0).astype(bf16)
    product = jnp.dot(spread, w1_own[...], preferred_element_type=f32)
    partial_out[...] = jnp.sum(product.reshape(requests, slots, units), axis=1)


def write_kernel(*refs):
    count = len(refs) // 2
    for copy in copies(list(zip(refs[:count], refs[count : 2 * count])), refs[-1]):
        copy.wait()


def score_kernel(own_ref, other_ref, w2_ref, head_ref, out_ref):
    pre_one = own_ref[...] + other_ref[...]
    hidden_one = (pre_one * sigmoid(pre_one)).astype(bf16)
    pre_two = jnp.dot(hidden_one, w2_ref[...], preferred_element_type=f32)
    hidden_two = (pre_two * sigmoid(pre_two)).astype(bf16)
    heads = jnp.broadcast_to(head_ref[...].astype(f32), (8, head_ref.shape[1])).astype(bf16)
    logit = lax.dot_general(heads, hidden_two, nt_dims, preferred_element_type=f32)
    out_ref[...] = logit[0:1]


def swap(value, axes, sizes, bits):
    shape = tuple(sizes[a] for a in axes)
    count = 1
    for size in shape:
        count *= size
    pairs = []
    for index in range(count):
        rest, coords = index, []
        for size in reversed(shape):
            coords.append(rest % size)
            rest //= size
        coords = coords[::-1]
        target = 0
        for coord, bit, size in zip(coords, bits, shape):
            target = target * size + (coord ^ bit)
        pairs.append((index, target))
    return lax.ppermute(value, axes, pairs)


def join(parts, turned=False):
    return kernel_call(
        functools.partial(join_kernel, turned),
        jax.ShapeDtypeStruct(parts[0].shape, bf16),
        [VMEM] * len(parts),
    )(*parts)


def reduce_rest(total, sizes, groups):
    parts = [total]
    bit = groups
    while bit < sizes["replica"]:
        total = join(parts) if len(parts) > 1 else total
        parts = [total, swap(total, ("replica",), sizes, (bit,))]
        bit *= 2
    bit = 1
    while bit < sizes["dp"]:
        total = join(parts) if len(parts) > 1 else total
        steps = [k * bit for k in range(1, 4) if k * bit < sizes["dp"]]
        parts = [total] + [swap(total, ("dp",), sizes, (k,)) for k in steps]
        bit *= 4
    return parts


def local(
    sizes,
    hot_slab,
    linear_state,
    square_state,
    serve_table,
    first_weight,
    second_weight,
    out_weight,
    step_blocks,
    feature_ids,
    click_labels,
    serve_layout,
    request_ids,
):
    owners = sizes["dp"]
    owned, half, rows = linear_state.shape
    steps, active = step_blocks.shape
    fresh = active // 2
    kept = active - fresh
    touched = active + fresh
    samples = feature_ids.shape[1] // sizes["mp"]
    slots, picks = feature_ids.shape[2:]
    units = first_weight.shape[2]
    ids = jnp.transpose(feature_ids, (0, 2, 3, 1))
    req = jnp.transpose(request_ids[0], (0, 2, 1))
    requests = req.shape[0]
    positions = owners * owned
    groups = 2 if sizes["replica"] > 1 else 1
    direct = owners == 4

    def struct(*shape, dtype=bf16):
        return jax.ShapeDtypeStruct(shape, dtype)

    w1_own = first_weight.reshape(-1, units)
    w1_other = swap(w1_own, ("mp",), sizes, (1,))
    slab_other = swap(hot_slab, ("mp",), sizes, (1,))
    head = out_weight.reshape(1, -1)
    serve_own = serve_table[0]

    lead = kernel_call(lead_kernel, struct(8, 128, dtype=f32), [], micros=20.0)()
    per = slots * picks
    note, pack, coded = kernel_call(
        open_kernel,
        (
            struct(steps * per + 8, samples, dtype=f32),
            struct(3 * owned, half, rows),
            struct(per + 8, samples, dtype=jnp.int32),
        ),
        [VMEM] * 6,
    )(lead, ids, click_labels, linear_state, square_state, serve_own)
    if direct:
        packs = [swap(pack, ("dp",), sizes, (k,)) for k in range(1, owners)]
    else:
        packs = [lax.all_gather(pack, "dp", axis=0, tiled=False)]
    coded = [swap(coded, ("replica",), sizes, (1,))] if groups > 1 else []
    counts_shape = struct(active * rows, slots * samples)
    others = struct(fresh, half, rows)
    share, rest_own, note_other = kernel_call(
        functools.partial(first_step_kernel, slots, picks, groups),
        (struct(2 * kept + fresh, half, rows), others, struct(*note.shape, dtype=f32)),
        [VMEM] * (7 + groups),
        [pltpu.VMEM(counts_shape.shape, bf16)] * groups,
    )(
        step_blocks,
        note,
        *coded,
        hot_slab,
        slab_other,
        w1_own,
        w1_other,
        second_weight,
        head,
    )
    notes = [note, note_other][:groups]
    share_turned = swap(share, ("mp",), sizes, (1,))
    late = lax.optimization_barrier((share, *packs))[1:]
    shared_shape = struct(kept, half, rows, dtype=f32)
    linear_old, square_old, weight_old, cross = kernel_call(
        functools.partial(shared_kernel, owners),
        (shared_shape, shared_shape, shared_shape, struct(3 * kept, half, rows, dtype=f32)),
        [VMEM] * (4 + len(packs)),
    )(step_blocks, linear_state, square_state, hot_slab, *late)
    cross, share_turned = lax.optimization_barrier((cross, share_turned))
    total = join([share, share_turned, rest_own], True)
    sums = early = reduce_rest(total, sizes, groups)
    cross = swap(cross, ("mp",), sizes, (1,))
    late = lax.optimization_barrier((total, *notes))[1:]
    counts = kernel_call(
        functools.partial(side_kernel, slots, picks, groups),
        (counts_shape,) * groups
        + (struct(2 * half, slots * samples, dtype=f32),) * groups,
        [VMEM] * (groups + 3),
    )(step_blocks, hot_slab, slab_other, *late)
    shared = struct(kept, half, rows)
    state_shape = struct(kept, half, rows, dtype=f32)
    payload = struct(active, half, rows)
    grad_own, grad_other, new_own, linear_mid, square_mid = kernel_call(
        functools.partial(second_step_kernel, slots, picks, groups, steps, len(sums)),
        (payload, payload, shared, state_shape, state_shape),
        [VMEM] * (9 + 3 * groups + len(sums)),
    )(
        step_blocks,
        *counts,
        *notes,
        *sums,
        linear_old,
        square_old,
        weight_old,
        cross,
        w1_own,
        w1_other,
        second_weight,
        head,
    )
    total = join([grad_own, swap(grad_other, ("mp",), sizes, (1,))])
    sums = reduce_rest(total, sizes, groups)
    late = lax.optimization_barrier((total, req))[1]
    wanted = kernel_call(
        functools.partial(wanted_kernel, rows), struct(positions * rows, requests * slots), [VMEM]
    )(late)
    late = lax.optimization_barrier((total, *packs))[1:]
    old_shape = struct(touched - kept, half, rows, dtype=f32)
    index_shape = struct(touched, 8, rows, dtype=jnp.int32)
    linear_old, square_old, weight_old, where, mine = kernel_call(
        functools.partial(state_kernel, owners),
        (old_shape, old_shape, old_shape, index_shape, index_shape),
        [VMEM] * (5 + len(packs)),
    )(step_blocks, serve_layout, linear_state, square_state, hot_slab, *late)
    results = (
        struct(*linear_state.shape, dtype=f32),
        struct(*square_state.shape, dtype=f32),
        struct(*serve_own.shape),
    )
    *results_at, partial = kernel_call(
        functools.partial(finish_kernel, owners, len(sums), len(early)),
        results + (struct(requests, units, dtype=f32),),
        [VMEM] * (13 + len(sums) + len(early) + len(packs)),
        [pltpu.VMEM((positions, half, rows), bf16)],
    )(
        linear_old,
        square_old,
        weight_old,
        where,
        mine,
        new_own,
        linear_mid,
        square_mid,
        wanted,
        w1_own,
        linear_state,
        square_state,
        serve_own,
        *sums,
        *early,
        *packs,
    )
    partial_other = swap(partial, ("mp",), sizes, (1,))
    linear_out, square_out, serve_out = kernel_call(
        write_kernel, results, [VMEM] * 3, [pltpu.SemaphoreType.DMA((3,))], (HBM, HBM, HBM)
    )(*results_at)
    scores = kernel_call(score_kernel, struct(1, requests, dtype=f32), [VMEM] * 4)(
        partial, partial_other, second_weight, head
    )
    return linear_out, square_out, serve_out[None], scores


def solution(mesh):
    sizes = dict(mesh.shape)
    placed = (
        P(None, "mp", None),
        P("dp", "mp", None),
        P("dp", "mp", None),
        P("replica", "dp", "mp", None),
        P(None, "mp", None),
        P(),
        P(),
        P("groups", None),
        P(None, ("groups", "dp", "replica"), None, None),
        P(None, ("groups", "dp", "replica")),
        P("replica", None),
        P("replica", ("groups", "dp"), None, None),
    )
    return jax.shard_map(
        functools.partial(local, sizes),
        mesh=mesh,
        in_specs=placed,
        out_specs=(
            P(("groups", "dp"), "mp", None),
            P(("groups", "dp"), "mp", None),
            P(("groups", "replica"), "dp", "mp", None),
            P("replica", ("groups", "dp")),
        ),
        check_vma=False,
    )
```
